256 devices in a mesh: utt: 8 (over y, core), tm: 32 (over z, x).
Axes of the slice: x: 4, y: 4, z: 8, core: 2. Of those that a mesh axis runs over, the one named last changes fastest.
Arguments:
- glu_out: bfloat16 [131072, 1536], P(('utt', 'tm')), may hold values from -6 to 6
- cotangent: bfloat16 [131072, 1536], P(('utt', 'tm')), may hold values from -12 to 12
- kernel: float32 [31, 1536], replicated, may hold values from -1 to 1
- conv_bias: float32 [1536], replicated, may hold values from -3 to 3
- out_weight: bfloat16 [1536, 1536], P('tm'), may hold values from -0.15625 to 0.15625
- blocks: int32 [8, 8], P('utt'), may hold values from 1 to 64, 128 in all within a row
- last_fill: int32 [8, 8], P('utt'), may hold values from 1 to 128
- noise_draws: float32 [8, 32, 1536], P(None, 'utt', 'tm'), may hold values from -6 to 6
- band_coef: float32 [8], replicated, may hold values from 0.05 to 1
Outputs:
- block_out: bfloat16 [131072, 1536], P(('utt', 'tm'))
- mean_grad: float32 [32, 1536], P('utt', 'tm')
The draws below stay inside these ranges and needn't reach their ends.
Inputs may be any that keep to these rules, and one draw needn't show every extreme that they name: Each row of blocks sums to exactly 128, and its largest entry is exactly 64.
All inputs are finite; a program needn't handle non-finite values.
Results may differ from the reference program's by a relative error of at most 0.0049.
Values may be sent and summed in bfloat16 or wider, within the bound.
No kernel may reach another device: no remote copies, remote signals or barrier semaphores. Data moves between devices by JAX's collectives and lax.ppermute only.
A program may use at most 64 MiB of HBM per device.

```python
import math
import jax
import jax.numpy as jnp
import numpy as np
from jax import lax

D = 1536
KW = 31
BLOCK = 128
BAND = 8
GROUPS = 8
GRP_BLK = 128
MOST = 64
UTT_GRP = 8
FRAMES = 131072


def draw_cotangent(key, part):
    key = jax.random.fold_in(key, 7)
    frame_key, shift_key = jax.random.split(key)
    channel_shift = jnp.clip(jax.random.normal(shift_key, (D,), jnp.float32), -6.0, 6.0)
    per_frame = jnp.clip(jax.random.normal(frame_key, (FRAMES, D), jnp.float32), -6.0, 6.0)
    result = per_frame + 0.25 * channel_shift[None, :]
    return result.astype(jnp.bfloat16)


def place_ends(values, key, smallest, top_value):
    extent = values.shape
    spot = [jax.random.randint(jax.random.fold_in(key, axis), (), 0, extent[axis]) for axis in range(len(extent))]
    values = values.at[tuple(spot)].set(smallest)
    longest = extent.index(max(extent))
    spot[longest] = (spot[longest] + 1) % extent[longest]
    return values.at[tuple(spot)].set(top_value)


def levels(own_key, extent, pieces, smallest, high):
    level, own = 1.0, jax.random.fold_in(own_key, 6)
    for axis_at, blocks in pieces:
        draws = jnp.exp(jax.random.uniform(jax.random.fold_in(own, axis_at), (blocks,), jnp.float32, smallest / len(pieces), high / len(pieces)))
        level = level * jnp.repeat(draws, extent[axis_at] // blocks).reshape([-1 if axis == axis_at else 1 for axis in range(len(extent))])
    return level


def profile(count, total, reach, lean):
    portions = [(1 << 20) // math.isqrt(rank ** lean) + 1 for rank in range(2, count + 1)]
    surplus, given = total - reach - (count - 1), [1] * (count - 1)
    while surplus > 0:
        free = [i for i in range(count - 1) if given[i] < reach]
        pool, remaining = sum([portions[i] for i in free]), surplus
        for i in free:
            addition = min(reach - given[i], max(1, remaining * portions[i] // pool), surplus)
            given[i] = given[i] + addition
            surplus = surplus - addition
    return np.array([reach] + given)


def ragged(rng, number_of, total, most, lean):
    if number_of == 2:
        one = jax.random.randint(rng, (), max(1, total - most), min(most, total - 1) + 1)
        return jnp.stack([one, total - one])
    tallies = jnp.asarray(profile(number_of, total, most, lean), jnp.int32)
    pairs = (number_of - 1) // 2
    giver, taker = tallies[1:1 + 2 * pairs:2], tallies[2:2 + 2 * pairs:2]
    room = jnp.minimum(giver - 1, most - taker)
    shifted = jax.random.randint(jax.random.fold_in(rng, 1), (pairs,), 0, 1 << 20) % (room + 1)
    tallies = tallies.at[1:1 + 2 * pairs:2].set(giver - shifted).at[2:2 + 2 * pairs:2].set(taker + shifted)
    return tallies[jax.random.permutation(jax.random.fold_in(rng, 2), number_of)]


def noise(key, extent, width, reach, cuts=(), kind=jnp.bfloat16):
    factor_of = levels(key, extent, cuts, -0.22, 0.18) if cuts else 1.0
    array = jax.random.normal(key, extent, jnp.float32) * width * factor_of
    return jnp.minimum(jnp.maximum(array, -reach), reach).astype(kind)


def setup_inputs(seed: int = 0) -> dict:
    keys = jax.random.split(jax.random.key(seed), 10)
    return {
        "glu_out": noise(keys[0], (FRAMES, D), 1.0, 6.0, ((0, 256),)),
        "cotangent": draw_cotangent(jax.random.fold_in(keys[9], 71), 0),
        "kernel": noise(keys[2], (KW, D), KW ** -0.5, 1.0, (), jnp.float32),
        "conv_bias": noise(keys[3], (D,), 0.5, 3.0, (), jnp.float32),
        "out_weight": noise(keys[4], (D, D), D ** -0.5, 0.15625, ((0, 32),)),
        "blocks": jax.vmap(lambda own: ragged(own, UTT_GRP, GRP_BLK, MOST, 2))(jax.random.split(keys[5], GROUPS)).reshape((GROUPS, UTT_GRP)).astype(jnp.int32),
        "last_fill": place_ends(jax.random.randint(keys[6], (GROUPS, UTT_GRP), 1, BLOCK + 1), jax.random.fold_in(keys[6], 1), 1, BLOCK).astype(jnp.int32),
        "noise_draws": noise(keys[7], (BAND, KW + 1, D), 1.0, 6.0, ((1, 8), (2, 32)), jnp.float32),
        "band_coef": jnp.clip(jnp.exp(jax.random.uniform(keys[8], (BAND,), jnp.float32, math.log(0.05), math.log(1.0))), 0.05, 1.0),
    }


def utt_ids(counts, blk_index):
    cumul = jnp.cumsum(counts).astype(jnp.int32)
    return lax.optimization_barrier(jnp.sum((cumul[None, :] <= blk_index[:, None]).astype(jnp.int32), axis=1, dtype=jnp.int32))

def utt_tables(counts, last_fills, blk_index):
    cumul = jnp.cumsum(counts).astype(jnp.int32)
    utt_of = utt_ids(counts, blk_index)
    chosen = (utt_of[:, None] == jnp.arange(counts.shape[0], dtype=jnp.int32)[None, :]).astype(jnp.int32)
    end_of = lax.optimization_barrier(jnp.sum(chosen * cumul[None, :], axis=1, dtype=jnp.int32))
    length_of = lax.optimization_barrier(jnp.sum(chosen * counts[None, :], axis=1, dtype=jnp.int32))
    fill_of = lax.optimization_barrier(jnp.sum(chosen * last_fills[None, :], axis=1, dtype=jnp.int32))
    return (utt_of, end_of, length_of, fill_of)

def frame_valid(blk_index, end_of, fill_of):
    limit = jnp.where(end_of - 1 == blk_index, fill_of, BLOCK)
    return jnp.arange(BLOCK, dtype=jnp.int32)[None, :] < limit[:, None]

def one_group(glu_grp, cot_grp, counts, last_fills, kernel, conv_bias, out_weight):
    rim_width = KW // 2
    frames = glu_grp.shape[0]
    blk_count = frames // BLOCK
    blk_index = jnp.arange(blk_count, dtype=jnp.int32)
    utt_of, end_of, length_of, fill_of = utt_tables(counts, last_fills, blk_index)
    valid_mask = frame_valid(blk_index, end_of, fill_of).reshape(frames)
    seg_ids = jnp.repeat(utt_of, BLOCK, total_repeat_length=frames)
    masked_in = glu_grp * valid_mask[:, None].astype(jnp.bfloat16)
    padded_in = jnp.pad(masked_in, ((rim_width, rim_width), (0, 0)))
    padded_seg = jnp.pad(seg_ids, (rim_width, rim_width), constant_values=-1)
    conv_out = jnp.zeros(glu_grp.shape, jnp.float32) + conv_bias[None, :]
    for tap_idx in range(KW):
        same_utt = (padded_seg[tap_idx:tap_idx + frames] == seg_ids).astype(jnp.float32)[:, None]
        conv_out = conv_out + kernel[tap_idx][None, :] * padded_in[tap_idx:tap_idx + frames].astype(jnp.float32) * same_utt
    keep_mask = valid_mask.astype(jnp.float32)[:, None]
    hidden = (jax.nn.silu(conv_out) * keep_mask).astype(jnp.bfloat16)
    block_out = jnp.dot(hidden, out_weight, preferred_element_type=jnp.float32).astype(jnp.bfloat16)
    hidden_grad = lax.dot_general(cot_grp, out_weight, (((1,), (1,)), ((), ())), preferred_element_type=jnp.float32)
    logistic = jax.nn.sigmoid(conv_out)
    conv_grad = hidden_grad * logistic * (1.0 + conv_out * (1.0 - logistic)) * keep_mask
    tap_rows = []
    for tap_idx in range(KW):
        same_utt = (padded_seg[tap_idx:tap_idx + frames] == seg_ids).astype(jnp.float32)[:, None]
        product = conv_grad * padded_in[tap_idx:tap_idx + frames].astype(jnp.float32) * same_utt
        tap_rows.append(lax.optimization_barrier(jnp.sum(product.reshape(blk_count, BLOCK, -1), axis=1)))
    tap_rows.append(lax.optimization_barrier(jnp.sum(conv_grad.reshape(blk_count, BLOCK, -1), axis=1)))
    block_grads = jnp.stack(tap_rows, axis=1)
    utt_grads = jax.ops.segment_sum(block_grads, utt_of, num_segments=counts.shape[0])
    grad_norm = jnp.sqrt(lax.optimization_barrier(jnp.sum(utt_grads * utt_grads, axis=(1, 2))))
    clip_bound = 300.0 * math.sqrt(D)
    factor = clip_bound / jnp.maximum(grad_norm, clip_bound)
    return (block_out, lax.optimization_barrier(jnp.sum(factor[:, None, None] * utt_grads, axis=0)))

def reference(glu_out, cotangent, kernel, conv_bias, out_weight, blocks, last_fill, noise_draws, band_coef):
    grp_frames = GRP_BLK * BLOCK
    glu_grp = glu_out.reshape(GROUPS, grp_frames, D)
    cot_grp = cotangent.reshape(GROUPS, grp_frames, D)

    def per_group(packed):
        return one_group(packed[0], packed[1], packed[2], packed[3], kernel, conv_bias, out_weight)
    outputs, clipped_sums = lax.map(per_group, (glu_grp, cot_grp, blocks, last_fill))
    summed = lax.optimization_barrier(jnp.sum(clipped_sums, axis=0))
    clip_bound = 300.0 * math.sqrt(D)
    mixture = lax.optimization_barrier(jnp.sum(band_coef[:, None, None] * noise_draws, axis=0))
    mean_grad = (summed + 0.1 * clip_bound * mixture) / (UTT_GRP * GROUPS)
    return (outputs.reshape(GROUPS * grp_frames, D), mean_grad)
```

```python
import math

import jax
import jax.numpy as jnp
from jax import lax
from jax.experimental import pallas as pl
from jax.experimental.pallas import tpu as pltpu
from jax.sharding import PartitionSpec as P

BLOCK = 128
LANES = 128
RIM = 16
PADDED = BLOCK + 2 * RIM
STEP = 256
TILES = STEP // LANES


def block_facts(counts, fills, utts, index):
    utt, limit, cumul = jnp.int32(0), jnp.int32(BLOCK), jnp.int32(0)
    for i in range(utts):
        cumul = cumul + counts[i]
        utt = utt + (cumul <= index).astype(jnp.int32)
        limit = jnp.where(cumul - 1 == index, fills[i], limit)
    return utt, limit


def conv_body(first, counts, fills, x, low, high, kernel, bias, hidden, slope, padded):
    taps = kernel.shape[0]
    frames = x.shape[0]
    blks = frames // BLOCK
    utts = counts.shape[0]
    facts = [block_facts(counts, fills, utts, first[0] + b) for b in range(-1, blks + 1)]
    row = lax.broadcasted_iota(jnp.int32, (BLOCK, LANES), 0)
    rim_row = lax.broadcasted_iota(jnp.int32, (RIM, LANES), 0)
    for tile in range(TILES):
        lanes = slice(tile * LANES, (tile + 1) * LANES)
        for b in range(blks):
            utt, limit = facts[b + 1]
            before = (facts[b][0] == utt) & (first[0] + b > 0)
            after = facts[b + 2][0] == utt
            keep = row < limit
            here = x[b * BLOCK : (b + 1) * BLOCK, lanes].astype(jnp.float32)
            left = low[:, lanes] if b == 0 else x[b * BLOCK - RIM : b * BLOCK, lanes]
            right = high[:, lanes] if b == blks - 1 else x[(b + 1) * BLOCK : (b + 1) * BLOCK + RIM, lanes]
            padded[tile, b, :RIM] = jnp.where(
                rim_row < jnp.where(before, RIM, 0), left.astype(jnp.float32), 0.0
            )
            padded[tile, b, RIM : RIM + BLOCK] = jnp.where(keep, here, 0.0)
            padded[tile, b, RIM + BLOCK :] = jnp.where(
                rim_row < jnp.where(after, facts[b + 2][1], 0), right.astype(jnp.float32), 0.0
            )
            total = jnp.broadcast_to(bias[:, lanes], (BLOCK, LANES))
            for k in range(taps):
                total = total + kernel[k : k + 1, lanes] * padded[tile, b, k + 1 : k + 1 + BLOCK]
            logistic = jax.nn.sigmoid(total)
            rows = slice(b * BLOCK, (b + 1) * BLOCK)
            hidden[rows, lanes] = jnp.where(keep, total * logistic, 0.0).astype(jnp.bfloat16)
            slope[rows, lanes] = jnp.where(
                keep, logistic * (1.0 + total * (1.0 - logistic)), 0.0
            )


def conv(first, counts, fills, x, low, high, kernel, bias):
    frames, width = x.shape
    blks = frames // BLOCK
    scalars = pl.BlockSpec(memory_space=pltpu.SMEM)
    column = lambda rows: pl.BlockSpec((rows, STEP), lambda c: (0, c))
    return pl.pallas_call(
        conv_body,
        grid=(width // STEP,),
        in_specs=[scalars] * 3
        + [column(frames), column(RIM), column(RIM), column(kernel.shape[0]), column(1)],
        out_specs=[
            column(frames),
            column(frames),
            pl.BlockSpec((TILES, blks, PADDED, LANES), lambda c: (c, 0, 0, 0)),
        ],
        out_shape=[
            jax.ShapeDtypeStruct((frames, width), jnp.bfloat16),
            jax.ShapeDtypeStruct((frames, width), jnp.float32),
            jax.ShapeDtypeStruct((width // LANES, blks, PADDED, LANES), jnp.float32),
        ],
        compiler_params=pltpu.CompilerParams(vmem_limit_bytes=24 << 20),
        cost_estimate=pl.CostEstimate(
            flops=2 * 31 * frames * width, bytes_accessed=12 * frames * width, transcendentals=frames * width
        ),
        name="conv",
    )(first, counts, fills, x, low, high, kernel, bias)


def grads_body(cot, weight, slope, padded, out, grad, parts):
    taps = 31
    blks = padded.shape[1]
    slots = 32
    hidden_grad = lax.dot_general(
        cot[...], weight[...], (((1,), (1,)), ((), ())), preferred_element_type=jnp.float32
    )
    for tile in range(TILES):
        lanes = slice(tile * LANES, (tile + 1) * LANES)
        grad[tile] = hidden_grad[:, lanes] * slope[:, lanes]
    for tile in range(TILES):
        for b in range(blks):
            own = grad[tile, b * BLOCK : (b + 1) * BLOCK]
            for k in range(taps + 1):
                term = own * padded[tile, b, k + 1 : k + 1 + BLOCK] if k < taps else own
                at = (b * slots + k) * 8
                parts[at : at + 8] = jnp.sum(term.reshape(BLOCK // 8, 8, LANES), axis=0)
        total = parts[pl.ds(0, blks * slots, stride=8)]
        for s in range(1, 8):
            total = total + parts[pl.ds(s, blks * slots, stride=8)]
        out[tile * LANES : (tile + 1) * LANES] = total.T.astype(out.dtype)


def grads(cot, weight, slope, padded):
    frames, width = cot.shape
    channels = weight.shape[0]
    blks = frames // BLOCK
    return pl.pallas_call(
        grads_body,
        grid=(channels // STEP,),
        in_specs=[
            pl.BlockSpec((frames, width), lambda c: (0, 0)),
            pl.BlockSpec((STEP, width), lambda c: (c, 0)),
            pl.BlockSpec((frames, STEP), lambda c: (0, c)),
            pl.BlockSpec((TILES, blks, PADDED, LANES), lambda c: (c, 0, 0, 0)),
        ],
        out_specs=pl.BlockSpec((STEP, blks * 32), lambda c: (c, 0)),
        out_shape=jax.ShapeDtypeStruct((channels, blks * 32), jnp.bfloat16),
        scratch_shapes=[
            pltpu.VMEM((TILES, frames, LANES), jnp.float32),
            pltpu.VMEM((blks * 32 * 8, LANES), jnp.float32),
        ],
        compiler_params=pltpu.CompilerParams(vmem_limit_bytes=32 << 20),
        cost_estimate=pl.CostEstimate(
            flops=2 * frames * width * channels, bytes_accessed=12 * frames * channels, transcendentals=0
        ),
        name="grads",
    )(cot, weight, slope, padded)


def sums_body(counts, parts, sums, norms):
    senders, channels, lanes = parts.shape
    utts = counts.shape[0]
    per = lanes // 32
    blk = lax.broadcasted_iota(jnp.int32, (senders, lanes), 0) * per + (
        lax.broadcasted_iota(jnp.int32, (senders, lanes), 1) // 32
    )
    utt_of, cumul = jnp.zeros((senders, lanes), jnp.int32), jnp.int32(0)
    for i in range(utts):
        cumul = cumul + counts[i]
        utt_of = utt_of + (cumul <= blk).astype(jnp.int32)
    spot = lax.broadcasted_iota(jnp.int32, (1, lanes), 1)
    row = jnp.zeros((1, lanes), jnp.float32)
    totals = [jnp.zeros((channels, lanes), jnp.float32) for _ in range(utts)]
    for s in range(senders):
        part = parts[s].astype(jnp.float32)
        owner = utt_of[s : s + 1]
        for u in range(utts):
            totals[u] = totals[u] + jnp.where(owner == u, part, 0.0)
    for u in range(utts):
        total = totals[u]
        total = total + pltpu.roll(total, 64, 1)
        total = total + pltpu.roll(total, 32, 1)
        sums[u] = total
        square = jnp.sum(jnp.sum(total * total, axis=0, keepdims=True), axis=1, keepdims=True)
        row = row + jnp.where(spot == u, square * (1.0 / per), 0.0)
    norms[...] = jnp.broadcast_to(row[None], norms.shape)


def sums_and_norms(counts, parts):
    senders, channels, lanes = parts.shape
    utts = counts.shape[0]
    vmem = pl.BlockSpec(memory_space=pltpu.VMEM)
    return pl.pallas_call(
        sums_body,
        in_specs=[pl.BlockSpec(memory_space=pltpu.SMEM), vmem],
        out_specs=[vmem, vmem],
        out_shape=[
            jax.ShapeDtypeStruct((utts, channels, lanes), jnp.float32),
            jax.ShapeDtypeStruct((senders, 1, lanes), jnp.float32),
        ],
        name="sums",
    )(counts, parts)


def clip_body(clip_bound, sums, norms, out):
    utts, channels, lanes = sums.shape
    square = jnp.sum(norms[...], axis=0)
    factor = clip_bound / jnp.maximum(jnp.sqrt(square), clip_bound)
    spot = lax.broadcasted_iota(jnp.int32, (1, lanes), 1)
    total = jnp.zeros((channels, lanes), jnp.float32)
    for u in range(utts):
        own = jnp.sum(jnp.where(spot == u, factor, 0.0), axis=1, keepdims=True)
        total = total + own * sums[u]
    wide = jnp.concatenate([total, jnp.zeros((lanes - channels, lanes), jnp.float32)], axis=0).T
    groups, rows, _ = out.shape
    for g in range(groups):
        out[g] = wide[g * rows : (g + 1) * rows]


def clipped(sums, norms, clip_bound, groups):
    vmem = pl.BlockSpec(memory_space=pltpu.VMEM)
    return pl.pallas_call(
        lambda *refs: clip_body(clip_bound, *refs),
        in_specs=[vmem, vmem],
        out_specs=vmem,
        out_shape=jax.ShapeDtypeStruct((groups, 32 // groups, LANES), jnp.float32),
        name="clip",
    )(sums, norms)


def per_device(
    glu_out, cotangent, kernel, conv_bias, out_weight, blocks, last_fill, noise_draws, band_coef
):
    frames, width = glu_out.shape
    blk_count = frames // BLOCK
    shards = lax.axis_size("tm")
    groups = lax.axis_size("utt")
    counts = blocks[0]
    fills = last_fill[0]
    first = (lax.axis_index("tm") * blk_count).astype(jnp.int32).reshape(1)
    full_weight = lax.all_gather(out_weight, "tm", axis=0, tiled=True)
    forward = [(i, i + 1) for i in range(shards - 1)]
    backward = [(target, source) for source, target in forward]
    low = lax.ppermute(glu_out[frames - RIM :], "tm", forward)
    high = lax.ppermute(glu_out[:RIM], "tm", backward)
    hidden, slope, padded = conv(first, counts, fills, glu_out, low, high, kernel, conv_bias[None])
    parts = grads(cotangent, full_weight, slope, padded)
    parts = lax.all_to_all(parts.reshape(shards, width // shards, parts.shape[1]), "tm", 0, 0, tiled=True)
    block_out = jnp.dot(hidden, full_weight, preferred_element_type=jnp.float32).astype(jnp.bfloat16)
    sums, norms = sums_and_norms(counts, parts)
    norms = lax.all_to_all(norms, "tm", 0, 0, tiled=True)
    clip_bound = 300.0 * math.sqrt(width)
    contrib = clipped(sums, norms, clip_bound, groups)
    contrib = lax.all_to_all(contrib, "utt", 0, 0, tiled=True)
    own_share = jnp.sum(contrib, axis=0)[:, : width // shards]
    mixture = jnp.sum(band_coef[:, None, None] * noise_draws, axis=0)
    mean_grad = (own_share + 0.1 * clip_bound * mixture) / (counts.shape[0] * groups)
    return (block_out, mean_grad)


def solution(mesh):
    return jax.shard_map(
        per_device,
        mesh=mesh,
        in_specs=(
            P(("utt", "tm"), None),
            P(("utt", "tm"), None),
            P(),
            P(),
            P("tm", None),
            P("utt", None),
            P("utt", None),
            P(None, "utt", "tm"),
            P(),
        ),
        out_specs=(P(("utt", "tm"), None), P("utt", "tm")),
        check_vma=False,
    )
```

```python
import math

import jax
import jax.numpy as jnp
from jax import lax
from jax.experimental import pallas as pl
from jax.experimental.pallas import tpu as pltpu
from jax.sharding import PartitionSpec as P

BLOCK = 128
LANES = 128
RIM = 16
PADDED = BLOCK + 2 * RIM
STEP = 256
PART = 384
SLOTS = 32
COLS = 4
UTTS = 8


def block_facts(scalars, utts, index):
    utt, limit, cumul = jnp.int32(0), jnp.int32(BLOCK), jnp.int32(0)
    for i in range(utts):
        cumul = cumul + scalars[i]
        utt = utt + (cumul <= index).astype(jnp.int32)
        limit = jnp.where(cumul - 1 == index, scalars[utts + i], limit)
    return utt, limit


def conv_body(
    scalars, x, low, high, kernel, bias, channel, hidden, slope, padded, stacked, picked
):
    taps = kernel.shape[0]
    frames, width = x.shape
    blks = frames // BLOCK

    @pl.when(pl.program_id(0) == 0)
    def _():
        stacked[:frames] = x[...]
        stacked[frames : frames + RIM] = low[...]
        stacked[frames + RIM : frames + 2 * RIM] = high[...]
        rest = jnp.concatenate([kernel[...], bias[...]], axis=0)
        for part in range(3):
            rounded = rest.astype(jnp.bfloat16)
            at = frames + 2 * RIM + part * (taps + 1)
            stacked[at : at + taps + 1] = rounded
            rest = rest - rounded.astype(jnp.float32)

    chosen = lax.broadcasted_iota(jnp.int32, (width, STEP), 0) == channel[...]
    picked[...] = jnp.dot(
        stacked[...],
        jnp.where(chosen, 1.0, 0.0).astype(jnp.bfloat16),
        preferred_element_type=jnp.float32,
    )
    first = scalars[2 * UTTS]
    facts = [block_facts(scalars, UTTS, first + b) for b in range(-1, blks + 1)]
    row = lax.broadcasted_iota(jnp.int32, (BLOCK, LANES), 0)
    rim_row = lax.broadcasted_iota(jnp.int32, (RIM, LANES), 0)
    for tile in range(STEP // LANES):
        lanes = slice(tile * LANES, (tile + 1) * LANES)
        at = frames + 2 * RIM
        weights = picked[at : at + taps + 1, lanes]
        for part in range(1, 3):
            at = at + taps + 1
            weights = weights + picked[at : at + taps + 1, lanes]
        for b in range(blks):
            utt, limit = facts[b + 1]
            before = (facts[b][0] == utt) & (first + b > 0)
            after = facts[b + 2][0] == utt
            keep = row < limit
            at = b * BLOCK
            here = picked[at : at + BLOCK, lanes]
            left = at - RIM if b else frames
            right = at + BLOCK if b < blks - 1 else frames + RIM
            padded[tile, b, :RIM] = jnp.where(
                rim_row < jnp.where(before, RIM, 0), picked[left : left + RIM, lanes], 0.0
            )
            padded[tile, b, RIM : RIM + BLOCK] = jnp.where(keep, here, 0.0)
            padded[tile, b, RIM + BLOCK :] = jnp.where(
                rim_row < jnp.where(after, facts[b + 2][1], 0),
                picked[right : right + RIM, lanes],
                0.0,
            )
            total = jnp.broadcast_to(weights[taps : taps + 1], (BLOCK, LANES))
            for k in range(taps):
                total = total + weights[k : k + 1] * padded[tile, b, k + 1 : k + 1 + BLOCK]
            logistic = jax.nn.sigmoid(total)
            rows = slice(at, at + BLOCK)
            hidden[rows, lanes] = jnp.where(keep, total * logistic, 0.0).astype(jnp.bfloat16)
            slope[rows, lanes] = jnp.where(
                keep, logistic * (1.0 + total * (1.0 - logistic)), 0.0
            )


def conv(scalars, x, low, high, kernel, bias, channel):
    frames, width = x.shape
    blks = frames // BLOCK
    stacked = frames + 2 * RIM + 3 * (kernel.shape[0] + 1)
    whole = lambda rows: pl.BlockSpec((rows, width), lambda c: (0, 0))
    column = lambda rows: pl.BlockSpec((rows, STEP), lambda c: (0, c))
    return pl.pallas_call(
        conv_body,
        grid=(width // STEP,),
        in_specs=[
            pl.BlockSpec(memory_space=pltpu.SMEM),
            whole(frames),
            whole(RIM),
            whole(RIM),
            whole(kernel.shape[0]),
            whole(1),
            column(1),
        ],
        out_specs=[
            column(frames),
            column(frames),
            pl.BlockSpec((STEP // LANES, blks, PADDED, LANES), lambda c: (c, 0, 0, 0)),
        ],
        out_shape=[
            jax.ShapeDtypeStruct((frames, width), jnp.bfloat16),
            jax.ShapeDtypeStruct((frames, width), jnp.float32),
            jax.ShapeDtypeStruct((width // LANES, blks, PADDED, LANES), jnp.float32),
        ],
        scratch_shapes=[
            pltpu.VMEM((stacked, width), jnp.bfloat16),
            pltpu.VMEM((stacked, STEP), jnp.float32),
        ],
        compiler_params=pltpu.CompilerParams(vmem_limit_bytes=24 << 20),
        cost_estimate=pl.CostEstimate(
            flops=2 * stacked * width * width, bytes_accessed=40 * frames * width, transcendentals=frames * width
        ),
        name="conv",
    )(scalars, x, low, high, kernel, bias, channel)


def tap_sums(own, padded, tile, b, parts):
    for k in range(SLOTS):
        term = own * padded[tile, b, k + 1 : k + 1 + BLOCK] if k < SLOTS - 1 else own
        at = (b * SLOTS + k) * 8
        parts[at : at + 8] = jnp.sum(term.reshape(BLOCK // 8, 8, LANES), axis=0)


def part_grads(cot, slope, padded, weight, grad, parts, store):
    blks = padded.shape[1]
    hidden_grad = lax.dot_general(
        cot[...], weight[...], (((1,), (1,)), ((), ())), preferred_element_type=jnp.float32
    )
    for tile in range(PART // LANES):
        lanes = slice(tile * LANES, (tile + 1) * LANES)
        grad[tile] = hidden_grad[:, lanes] * slope[:, lanes]
    for tile in range(PART // LANES):
        for b in range(blks):
            tap_sums(grad[tile, b * BLOCK : (b + 1) * BLOCK], padded, tile, b, parts)
        total = parts[pl.ds(0, blks * SLOTS, stride=8)]
        for s in range(1, 8):
            total = total + parts[pl.ds(s, blks * SLOTS, stride=8)]
        store(tile, total.T)


def early_body(pieces, cot, slope, padded, *rest):
    rows, out, weight, grad, parts = rest[:-4], rest[-4], rest[-3], rest[-2], rest[-1]
    per = len(rows) // pieces
    for step in range(pieces):

        @pl.when(pl.program_id(0) == step)
        def _():
            at = 0
            for piece in rows[step * per : (step + 1) * per]:
                weight[at : at + piece.shape[0]] = piece[...]
                at = at + piece.shape[0]

    def store(tile, value):
        out[tile * LANES : (tile + 1) * LANES] = value

    part_grads(cot, slope, padded, weight, grad, parts, store)


def last_body(scalars, early, middle, cot, slope, padded, *rest):
    rows, out, late, weight, grad, parts = rest[:-5], rest[-5], rest[-4], rest[-3], rest[-2], rest[-1]
    at = 0
    for piece in rows:
        weight[at : at + piece.shape[0]] = piece[...]
        at = at + piece.shape[0]

    def store(tile, value):
        late[tile * LANES : (tile + 1) * LANES] = value

    part_grads(cot, slope, padded, weight, grad, parts, store)
    col, core = scalars[2 * UTTS + 1], scalars[2 * UTTS + 2]
    half = PART // 2
    share = out.shape[1] // 2
    depth = half // share
    for ref, base, shift in ((early, 0, 0), (middle, 0, COLS - 1), (middle, PART, 1), (late, 0, 2)):
        target = lax.rem(col + shift, COLS)
        for z in range(depth):
            mine = ref[base + z * share : base + (z + 1) * share]
            other = ref[base + half + z * share : base + half + (z + 1) * share]
            is_first = core == 0
            both = jnp.concatenate(
                [jnp.where(is_first, mine, other), jnp.where(is_first, other, mine)], axis=0
            )
            out[z * COLS + target] = both.astype(out.dtype)


def grad_scratch(frames, width, blks):
    return [
        pltpu.VMEM((PART, width), jnp.bfloat16),
        pltpu.VMEM((PART // LANES, frames, LANES), jnp.float32),
        pltpu.VMEM((blks * SLOTS * 8, LANES), jnp.float32),
    ]


def grad_cost(frames, width, channels):
    return pl.CostEstimate(
        flops=2 * frames * width * channels, bytes_accessed=20 * frames * channels, transcendentals=0
    )


def early_grads(cot, slope, padded, rows, start):
    frames, width = cot.shape
    blks = frames // BLOCK
    channels = sum(piece.shape[0] for piece in rows)
    steps = channels // PART
    return pl.pallas_call(
        lambda *refs: early_body(steps, *refs),
        grid=(steps,),
        in_specs=[
            pl.BlockSpec((frames, width), lambda c: (0, 0)),
            pl.BlockSpec((frames, PART), lambda c: (0, c + start)),
            pl.BlockSpec((PART // LANES, blks, PADDED, LANES), lambda c: (c + start, 0, 0, 0)),
        ]
        + [pl.BlockSpec(piece.shape, lambda c: (0, 0)) for piece in rows],
        out_specs=pl.BlockSpec((PART, blks * SLOTS), lambda c: (c, 0)),
        out_shape=jax.ShapeDtypeStruct((channels, blks * SLOTS), jnp.float32),
        scratch_shapes=grad_scratch(frames, width, blks),
        compiler_params=pltpu.CompilerParams(vmem_limit_bytes=24 << 20),
        cost_estimate=grad_cost(frames, width, channels),
        name="grads",
    )(cot, slope, padded, *rows)


def last_grads(scalars, early, middle, cot, slope, padded, rows, start, shards):
    frames, width = cot.shape
    blks = frames // BLOCK
    channels = sum(piece.shape[0] for piece in rows)
    return pl.pallas_call(
        last_body,
        grid=(1,),
        in_specs=[
            pl.BlockSpec(memory_space=pltpu.SMEM),
            pl.BlockSpec(early.shape, lambda c: (0, 0)),
            pl.BlockSpec(middle.shape, lambda c: (0, 0)),
            pl.BlockSpec((frames, width), lambda c: (0, 0)),
            pl.BlockSpec((frames, PART), lambda c: (0, start)),
            pl.BlockSpec((PART // LANES, blks, PADDED, LANES), lambda c: (start, 0, 0, 0)),
        ]
        + [pl.BlockSpec(piece.shape, lambda c: (0, 0)) for piece in rows],
        out_specs=pl.BlockSpec((shards, width // shards, blks * SLOTS), lambda c: (0, 0, 0)),
        out_shape=jax.ShapeDtypeStruct((shards, width // shards, blks * SLOTS), jnp.bfloat16),
        scratch_shapes=[pltpu.VMEM((PART, blks * SLOTS), jnp.float32)]
        + grad_scratch(frames, width, blks),
        compiler_params=pltpu.CompilerParams(vmem_limit_bytes=24 << 20),
        cost_estimate=grad_cost(frames, width, channels),
        name="last_grads",
    )(scalars, early, middle, cot, slope, padded, *rows)


def project_body(hidden, *rest):
    rows, out, weight = rest[:-2], rest[-2], rest[-1]

    @pl.when(pl.program_id(0) == 0)
    def _():
        at = 0
        for piece in rows:
            weight[at : at + piece.shape[0]] = piece[...]
            at = at + piece.shape[0]

    step = out.shape[1]
    lanes = pl.ds(pl.multiple_of(pl.program_id(0) * step, step), step)
    out[...] = jnp.dot(
        hidden[...], weight[:, lanes], preferred_element_type=jnp.float32
    ).astype(out.dtype)


def project(hidden, rows):
    frames, width = hidden.shape
    step = 512
    return pl.pallas_call(
        project_body,
        grid=(width // step,),
        in_specs=[pl.BlockSpec(hidden.shape, lambda c: (0, 0))]
        + [pl.BlockSpec(piece.shape, lambda c: (0, 0), pipeline_mode=pl.Buffered(1)) for piece in rows],
        out_specs=pl.BlockSpec((frames, step), lambda c: (0, c)),
        out_shape=jax.ShapeDtypeStruct((frames, width), jnp.bfloat16),
        scratch_shapes=[pltpu.VMEM((width, width), jnp.bfloat16)],
        compiler_params=pltpu.CompilerParams(vmem_limit_bytes=28 << 20),
        cost_estimate=pl.CostEstimate(
            flops=2 * frames * width * width, bytes_accessed=2 * width * width + 4 * frames * width, transcendentals=0
        ),
        name="project",
    )(hidden, *rows)


def sums_body(scalars, parts, sums, norms):
    senders, channels, lanes = parts.shape
    utts = UTTS
    per = lanes // SLOTS
    blk = lax.broadcasted_iota(jnp.int32, (senders, lanes), 0) * per + (
        lax.broadcasted_iota(jnp.int32, (senders, lanes), 1) // SLOTS
    )
    utt_of, cumul = jnp.zeros((senders, lanes), jnp.int32), jnp.int32(0)
    for i in range(utts):
        cumul = cumul + scalars[i]
        utt_of = utt_of + (cumul <= blk).astype(jnp.int32)
    spot = lax.broadcasted_iota(jnp.int32, (1, lanes), 1)
    row = jnp.zeros((1, lanes), jnp.float32)
    totals = [jnp.zeros((channels, lanes), jnp.float32) for _ in range(utts)]
    for s in range(senders):
        part = parts[s].astype(jnp.float32)
        owner = utt_of[s : s + 1]
        for u in range(utts):
            totals[u] = totals[u] + jnp.where(owner == u, part, 0.0)
    for u in range(utts):
        total = totals[u]
        total = total + pltpu.roll(total, 64, 1)
        total = total + pltpu.roll(total, 32, 1)
        sums[u] = total
        square = jnp.sum(jnp.sum(total * total, axis=0, keepdims=True), axis=1, keepdims=True)
        row = row + jnp.where(spot == u, square * (1.0 / per), 0.0)
    norms[...] = jnp.broadcast_to(row[None], norms.shape)


def sums_and_norms(scalars, parts):
    senders, channels, lanes = parts.shape
    utts = UTTS
    vmem = pl.BlockSpec(memory_space=pltpu.VMEM)
    return pl.pallas_call(
        sums_body,
        in_specs=[pl.BlockSpec(memory_space=pltpu.SMEM), vmem],
        out_specs=[vmem, vmem],
        out_shape=[
            jax.ShapeDtypeStruct((utts, channels, lanes), jnp.float32),
            jax.ShapeDtypeStruct((senders, 1, lanes), jnp.float32),
        ],
        name="sums",
    )(scalars, parts)


def clip_body(clip_bound, sums, norms, out):
    utts, channels, lanes = sums.shape
    square = jnp.sum(norms[...], axis=0)
    factor = clip_bound / jnp.maximum(jnp.sqrt(square), clip_bound)
    spot = lax.broadcasted_iota(jnp.int32, (1, lanes), 1)
    total = jnp.zeros((channels, lanes), jnp.float32)
    for u in range(utts):
        own = jnp.sum(jnp.where(spot == u, factor, 0.0), axis=1, keepdims=True)
        total = total + own * sums[u]
    wide = jnp.concatenate([total, jnp.zeros((lanes - channels, lanes), jnp.float32)], axis=0).T
    groups, rows, _ = out.shape
    for g in range(groups):
        out[g] = wide[g * rows : (g + 1) * rows]


def clipped(sums, norms, clip_bound, groups):
    vmem = pl.BlockSpec(memory_space=pltpu.VMEM)
    return pl.pallas_call(
        lambda *refs: clip_body(clip_bound, *refs),
        in_specs=[vmem, vmem],
        out_specs=vmem,
        out_shape=jax.ShapeDtypeStruct((groups, SLOTS // groups, LANES), jnp.float32),
        name="clip",
    )(sums, norms)


def gathered_rows(out_weight, core, shards, groups):
    depth = shards // COLS
    half = out_weight.shape[0] // 2
    width = out_weight.shape[1]
    mate = [(i, i ^ 1) for i in range(groups)]

    def shifted(value, by):
        pairs = [(z * COLS + x, z * COLS + (x + by) % COLS) for z in range(depth) for x in range(COLS)]
        return lax.ppermute(value, "tm", pairs)

    def swapped(value):
        return lax.ppermute(value, "utt", mate)

    def flat(value):
        return value.reshape(-1, width)

    own = lax.dynamic_slice_in_dim(out_weight, core * half, half, axis=0)
    own = lax.all_to_all(
        jnp.broadcast_to(own[None], (depth, half, width)),
        "tm",
        0,
        0,
        axis_index_groups=[[z * COLS + x for z in range(depth)] for x in range(COLS)],
        tiled=True,
    )
    below, above = shifted(own, 1), shifted(own, -1)
    own_mate = swapped(own)
    far_low, far_high = shifted(below[: depth // 2], 1), shifted(above[depth // 2 :], -1)
    below_mate, above_mate = swapped(below), swapped(above)
    far_low_mate, far_high_mate = swapped(far_low), swapped(far_high)
    return (
        [flat(own), flat(own_mate)],
        [flat(below), flat(below_mate), flat(above), flat(above_mate)],
        [flat(far_low), flat(far_high), flat(far_low_mate), flat(far_high_mate)],
    )


def arrival_channels(col, core, shards, width):
    depth = shards // COLS
    half = width // shards // 2
    place = jnp.arange(width, dtype=jnp.int32)
    inner = place % half
    z = place // half % depth
    mate = place // (half * depth) % 2
    side = place // (half * depth * 2)
    shift = jnp.where(side == 1, COLS - 1, jnp.where(side == 2, 1, jnp.where(side == 3, 2, 0)))
    x = (col + shift) % COLS
    return ((z * COLS + x) * 2 + (core ^ mate)) * half + inner


def per_device(
    glu_out, cotangent, kernel, conv_bias, out_weight, blocks, last_fill, noise_draws, band_coef
):
    frames, width = glu_out.shape
    blk_count = frames // BLOCK
    shards = lax.axis_size("tm")
    groups = lax.axis_size("utt")
    device = lax.axis_index("tm").astype(jnp.int32)
    core = lax.axis_index("utt").astype(jnp.int32) % 2
    col = device % COLS
    scalars = jnp.concatenate(
        [blocks[0], last_fill[0], jnp.stack([device * blk_count, col, core])]
    )
    near, sides, far = gathered_rows(out_weight, core, shards, groups)
    forward = [(i, i + 1) for i in range(shards - 1)]
    backward = [(target, source) for source, target in forward]
    low = lax.ppermute(glu_out[frames - RIM :], "tm", forward)
    high = lax.ppermute(glu_out[:RIM], "tm", backward)
    channel = arrival_channels(col, core, shards, width)[None]
    hidden, slope, padded = conv(scalars, glu_out, low, high, kernel, conv_bias[None], channel)
    early = early_grads(cotangent, slope, padded, near, 0)
    middle = early_grads(cotangent, slope, padded, sides, 1)
    parts = last_grads(scalars, early, middle, cotangent, slope, padded, far, 3, shards)
    parts = lax.all_to_all(parts, "tm", 0, 0, tiled=True)
    block_out = project(hidden, near + sides + far)
    sums, norms = sums_and_norms(scalars, parts)
    norms = lax.all_to_all(norms, "tm", 0, 0, tiled=True)
    clip_bound = 300.0 * math.sqrt(width)
    contrib = clipped(sums, norms, clip_bound, groups)
    contrib = lax.all_to_all(contrib, "utt", 0, 0, tiled=True)
    own_share = jnp.sum(contrib, axis=0)[:, : width // shards]
    mixture = jnp.sum(band_coef[:, None, None] * noise_draws, axis=0)
    mean_grad = (own_share + 0.1 * clip_bound * mixture) / (UTTS * groups)
    return (block_out, mean_grad)


def solution(mesh):
    return jax.shard_map(
        per_device,
        mesh=mesh,
        in_specs=(
            P(("utt", "tm"), None),
            P(("utt", "tm"), None),
            P(),
            P(),
            P("tm", None),
            P("utt", None),
            P("utt", None),
            P(None, "utt", "tm"),
            P(),
        ),
        out_specs=(P(("utt", "tm"), None), P("utt", "tm")),
        check_vma=False,
    )
```

```python
import math

import jax
import jax.numpy as jnp
from jax import lax
from jax.experimental import pallas as pl
from jax.experimental.pallas import tpu as pltpu
from jax.sharding import PartitionSpec as P

BLOCK = 128
LANES = 128
RIM = 16
PADDED = BLOCK + 2 * RIM
STEP = 384
SLOTS = 32
COLS = 4
UTTS = 8
VMEM = 60 << 20


def block_facts(scalars, utts, index):
    utt, limit, cumul = jnp.int32(0), jnp.int32(BLOCK), jnp.int32(0)
    for i in range(utts):
        cumul = cumul + scalars[i]
        utt = utt + (cumul <= index).astype(jnp.int32)
        limit = jnp.where(cumul - 1 == index, scalars[utts + i], limit)
    return utt, limit


def conv_body(blks, scalars, x, *rest):
    rims, (kernel, bias, hidden, slope, padded) = rest[:-5], rest[-5:]
    count = x.shape[0] // BLOCK
    first = scalars[2 * UTTS]
    row = lax.broadcasted_iota(jnp.int32, (BLOCK, LANES), 0)
    rim_row = lax.broadcasted_iota(jnp.int32, (RIM, LANES), 0)
    facts = {}
    for b in blks:
        for near in (b - 1, b, b + 1):
            if near not in facts:
                facts[near] = block_facts(scalars, UTTS, first + near)
    for tile in range(STEP // LANES):
        lanes = slice(tile * LANES, (tile + 1) * LANES)
        for i, b in enumerate(blks):
            utt, limit = facts[b]
            before = (facts[b - 1][0] == utt) & (first + b > 0)
            after = facts[b + 1][0] == utt
            keep = row < limit
            at = b * BLOCK
            left = x[at - RIM : at, lanes] if b else rims[0][:, lanes]
            right = x[at + BLOCK : at + BLOCK + RIM, lanes] if b < count - 1 else rims[1][:, lanes]
            pad = padded.at[tile, i]
            pad[:RIM] = jnp.where(
                rim_row < jnp.where(before, RIM, 0), left.astype(jnp.float32), 0.0
            )
            pad[RIM : RIM + BLOCK] = jnp.where(
                keep, x[at : at + BLOCK, lanes].astype(jnp.float32), 0.0
            )
            pad[RIM + BLOCK :] = jnp.where(
                rim_row < jnp.where(after, facts[b + 1][1], 0), right.astype(jnp.float32), 0.0
            )
            total = jnp.broadcast_to(bias[:, lanes], (BLOCK, LANES))
            for window, taps in windows(pad):
                for q, k in taps:
                    total = total + kernel[k : k + 1, lanes] * window[8 * q : 8 * q + BLOCK]
            logistic = jax.nn.sigmoid(total)
            to = slice(i * BLOCK, (i + 1) * BLOCK)
            hidden[to, lanes] = jnp.where(keep, total * logistic, 0.0).astype(jnp.bfloat16)
            slope[tile, to] = jnp.where(
                keep, logistic * (1.0 + total * (1.0 - logistic)), 0.0
            ).astype(jnp.bfloat16)


def conv(blks, scalars, x, rims, kernel, bias):
    frames, width = x.shape
    own = len(blks) * BLOCK
    column = lambda rows: pl.BlockSpec((rows, STEP), lambda c: (0, c))
    return pl.pallas_call(
        lambda *refs: conv_body(blks, *refs),
        grid=(width // STEP,),
        in_specs=[pl.BlockSpec(memory_space=pltpu.SMEM), column(frames)]
        + [column(RIM)] * len(rims)
        + [column(kernel.shape[0]), column(1)],
        out_specs=[
            column(own),
            pl.BlockSpec((STEP // LANES, own, LANES), lambda c: (c, 0, 0)),
            pl.BlockSpec((STEP // LANES, len(blks), PADDED, LANES), lambda c: (c, 0, 0, 0)),
        ],
        out_shape=[
            jax.ShapeDtypeStruct((own, width), jnp.bfloat16),
            jax.ShapeDtypeStruct((width // LANES, own, LANES), jnp.bfloat16),
            jax.ShapeDtypeStruct((width // LANES, len(blks), PADDED, LANES), jnp.float32),
        ],
        compiler_params=pltpu.CompilerParams(vmem_limit_bytes=VMEM),
        cost_estimate=pl.CostEstimate(
            flops=64 * own * width, bytes_accessed=40 * own * width, transcendentals=own * width
        ),
        name="conv",
    )(scalars, x, *rims, kernel, bias)


class Rows:
    def __init__(self, own, below, above, far_low, far_high):
        self.pieces = [*own, *below, *above, *far_low, *far_high]

    def copies(self, scalars, pieces, weight, sems, part):
        col, core = scalars[2 * UTTS + 1], scalars[2 * UTTS + 2]
        mid, half = pieces[0].shape[0] // 2, pieces[0].shape[2]
        rows = pl.ds(part * mid, mid)
        found = []
        for i in range(2 * COLS):
            piece = pieces[i + 2 * part].at[...] if i >= 6 else pieces[i].at[rows]
            side = 1 - core if i % 2 else core
            shift = (0, COLS - 1, 1, 2)[i // 2]
            found.append(
                pltpu.make_async_copy(
                    piece,
                    weight.at[
                        rows,
                        lax.rem(col + shift, COLS),
                        :,
                        pl.ds(pl.multiple_of(side * half, half), half),
                    ],
                    sems.at[part, i],
                )
            )
        return found

    def scratch(self):
        depth, run, half = self.pieces[0].shape
        return [
            pltpu.VMEM((depth, COLS, run, 2 * half), jnp.bfloat16),
            pltpu.SemaphoreType.DMA((2, 2 * COLS)),
        ]

    def specs(self):
        return [pl.BlockSpec(memory_space=pl.ANY)] * len(self.pieces)


def windows(pad):
    for shift in range(8):
        taps = [(q, 8 * q + shift - 1) for q in range(4) if 0 <= 8 * q + shift - 1 < SLOTS - 1]
        yield pad[shift : shift + BLOCK + 24], taps


def tap_sums(own, pad, b, parts):
    def keep(k, term):
        at = (b * SLOTS + k) * 8
        parts[at : at + 8] = jnp.sum(term.reshape(BLOCK // 8, 8, LANES), axis=0)

    for window, taps in windows(pad):
        for q, k in taps:
            keep(k, own * window[8 * q : 8 * q + BLOCK])
    keep(SLOTS - 1, own)


def grads_body(whole, orders, scalars, cot_far, *rest):
    count = len(orders)
    far, rest = rest[: 2 * count], rest[2 * count :]
    pieces, rest = rest[: len(whole.pieces)], rest[len(whole.pieces) :]
    out, weight, row_sems, cot, *rest = rest
    near, (grad, parts, sems) = rest[: 2 * count], rest[2 * count :]
    depth, cols, run, width = weight.shape
    blks = cot.shape[0] // BLOCK
    steps = 2
    per = depth // steps
    wide_step = per * cols * run
    tiles = wide_step // LANES
    row_copies = [whole.copies(scalars, pieces, weight, row_sems, i) for i in range(steps)]
    head = 3
    first, later = [], []
    for i, (source, target) in enumerate(zip(far, near)):
        for j, (found, low, high) in enumerate(((first, 0, head), (later, head, source.shape[0]))):
            found.append(
                pltpu.make_async_copy(source.at[low:high], target.at[low:high], sems.at[2 * i + j])
            )
    cot_copy = pltpu.make_async_copy(cot_far, cot, sems.at[2 * len(far)])
    for copy in [cot_copy] + row_copies[0]:
        copy.start()

    def taps(step, tile):
        column = step * tiles + tile
        for h, order in enumerate(orders):
            slope, padded = near[2 * h], near[2 * h + 1]
            for i, b in enumerate(order):
                factor = slope[column, i * BLOCK : (i + 1) * BLOCK].astype(jnp.float32)
                tap_sums(grad[tile, b * BLOCK : (b + 1) * BLOCK] * factor, padded.at[column, i], b, parts.at[tile])
        total = parts[tile, pl.ds(0, blks * SLOTS, stride=8)]
        for s in range(1, 8):
            total = total + parts[tile, pl.ds(s, blks * SLOTS, stride=8)]
        out[pl.ds(pl.multiple_of(column * LANES, LANES), LANES)] = total.T.astype(out.dtype)

    def one(step, carry):
        @pl.when(step == 0)
        def _():
            for copy in [cot_copy] + row_copies[0]:
                copy.wait()
            for copy in first + later + row_copies[1]:
                copy.start()

        @pl.when(step == 1)
        def _():
            for copy in row_copies[1]:
                copy.wait()

        hidden_grad = lax.dot_general(
            cot[...],
            weight[pl.ds(step * per, per)].reshape(wide_step, width),
            (((1,), (1,)), ((), ())),
            preferred_element_type=jnp.float32,
        )
        for tile in range(tiles):
            grad[tile] = hidden_grad[:, tile * LANES : (tile + 1) * LANES]

        for low, high, copies in ((0, head, first), (head, tiles, later)):

            @pl.when(step == 0)
            def _():
                for copy in copies:
                    copy.wait()

            for tile in range(low, high):
                taps(step, tile)
        return carry

    lax.fori_loop(0, steps, one, 0)


def grads(scalars, cot, halves, whole):
    frames, width = cot.shape
    blks = frames // BLOCK
    orders = [half[0] for half in halves]
    arrays = [array for half in halves for array in half[1:]]
    anywhere = pl.BlockSpec(memory_space=pl.ANY)
    return pl.pallas_call(
        lambda *refs: grads_body(whole, orders, *refs),
        in_specs=[pl.BlockSpec(memory_space=pltpu.SMEM), anywhere] + [anywhere] * len(arrays) + whole.specs(),
        out_specs=pl.BlockSpec(memory_space=pltpu.VMEM),
        out_shape=jax.ShapeDtypeStruct((width, blks * SLOTS), jnp.bfloat16),
        scratch_shapes=whole.scratch()
        + [pltpu.VMEM(array.shape, array.dtype) for array in [cot] + arrays]
        + [
            pltpu.VMEM((width // 2 // LANES, frames, LANES), jnp.float32),
            pltpu.VMEM((width // 2 // LANES, blks * SLOTS * 8, LANES), jnp.float32),
            pltpu.SemaphoreType.DMA((1 + 2 * len(arrays),)),
        ],
        compiler_params=pltpu.CompilerParams(vmem_limit_bytes=VMEM),
        cost_estimate=pl.CostEstimate(
            flops=2 * frames * width * width, bytes_accessed=20 * frames * width, transcendentals=0
        ),
        name="grads",
    )(scalars, cot, *arrays, *whole.pieces)


def project_body(whole, orders, scalars, *refs):
    hiddens, rest = refs[: len(orders)], refs[len(orders) :]
    pieces, (out, weight, sems) = rest[:-3], rest[-3:]

    @pl.when(pl.program_id(0) == 0)
    def _():
        found = [copy for part in range(2) for copy in whole.copies(scalars, pieces, weight, sems, part)]
        for copy in found:
            copy.start()
        for copy in found:
            copy.wait()

    step = out.shape[1]
    lanes = pl.ds(pl.multiple_of(pl.program_id(0) * step, step), step)
    for order, hidden in zip(orders, hiddens):
        product = jnp.dot(
            hidden[...],
            weight[:, :, :, lanes].reshape(hidden.shape[1], step),
            preferred_element_type=jnp.float32,
        )
        for i, b in enumerate(order):
            out[b * BLOCK : (b + 1) * BLOCK] = product[i * BLOCK : (i + 1) * BLOCK].astype(out.dtype)


def project(scalars, orders, hiddens, whole):
    width = hiddens[0].shape[1]
    frames = sum(hidden.shape[0] for hidden in hiddens)
    step = 512
    return pl.pallas_call(
        lambda *refs: project_body(whole, orders, *refs),
        grid=(width // step,),
        in_specs=[pl.BlockSpec(memory_space=pltpu.SMEM)]
        + [pl.BlockSpec(hidden.shape, lambda c: (0, 0)) for hidden in hiddens]
        + whole.specs(),
        out_specs=pl.BlockSpec((frames, step), lambda c: (0, c)),
        out_shape=jax.ShapeDtypeStruct((frames, width), jnp.bfloat16),
        scratch_shapes=whole.scratch(),
        compiler_params=pltpu.CompilerParams(vmem_limit_bytes=VMEM),
        cost_estimate=pl.CostEstimate(
            flops=2 * frames * width * width, bytes_accessed=2 * width * width + 4 * frames * width, transcendentals=0
        ),
        name="project",
    )(scalars, *hiddens, *whole.pieces)


def sums_body(scalars, parts, sums, norms, chosen):
    senders, channels, lanes = parts.shape
    utts = UTTS
    per = lanes // SLOTS
    blk = lax.broadcasted_iota(jnp.int32, (senders, lanes), 0) * per + (
        lax.broadcasted_iota(jnp.int32, (senders, lanes), 1) // SLOTS
    )
    utt_of, cumul = jnp.zeros((senders, lanes), jnp.int32), jnp.int32(0)
    for i in range(utts):
        cumul = cumul + scalars[i]
        utt_of = utt_of + (cumul <= blk).astype(jnp.int32)
    for u in range(utts):
        chosen[u] = jnp.where(utt_of == u, 1.0, 0.0)
    spot = lax.broadcasted_iota(jnp.int32, (1, lanes), 1)
    row = jnp.zeros((1, lanes), jnp.float32)
    totals = [jnp.zeros((channels, lanes), jnp.float32) for _ in range(utts)]
    for s in range(senders):
        part = parts[s].astype(jnp.float32)
        for u in range(utts):
            totals[u] = totals[u] + chosen[u, s : s + 1] * part
    for u in range(utts):
        total = totals[u]
        total = total + pltpu.roll(total, 64, 1)
        total = total + pltpu.roll(total, 32, 1)
        sums[u] = total
        square = jnp.sum(jnp.sum(total * total, axis=0, keepdims=True), axis=1, keepdims=True)
        row = row + jnp.where(spot == u, square * (1.0 / per), 0.0)
    norms[...] = jnp.broadcast_to(row[None], norms.shape)


def sums_and_norms(scalars, parts):
    senders, channels, lanes = parts.shape
    whole = lambda shape: pl.BlockSpec(shape, lambda c: (0, 0, 0))
    return pl.pallas_call(
        sums_body,
        grid=(1,),
        in_specs=[pl.BlockSpec(memory_space=pltpu.SMEM), whole(parts.shape)],
        out_specs=[whole((UTTS, channels, lanes)), whole((senders, 1, lanes))],
        out_shape=[
            jax.ShapeDtypeStruct((UTTS, channels, lanes), jnp.float32),
            jax.ShapeDtypeStruct((senders, 1, lanes), jnp.float32),
        ],
        scratch_shapes=[pltpu.VMEM((UTTS, senders, lanes), jnp.float32)],
        name="sums",
    )(scalars, parts)


def clip_body(clip_bound, sums, norms, out):
    utts, channels, lanes = sums.shape
    square = jnp.sum(norms[...], axis=0)
    factor = clip_bound / jnp.maximum(jnp.sqrt(square), clip_bound)
    spot = lax.broadcasted_iota(jnp.int32, (1, lanes), 1)
    total = jnp.zeros((channels, lanes), jnp.float32)
    for u in range(utts):
        own = jnp.sum(jnp.where(spot == u, factor, 0.0), axis=1, keepdims=True)
        total = total + own * sums[u]
    wide = jnp.concatenate([total, jnp.zeros((lanes - channels, lanes), jnp.float32)], axis=0).T
    groups, rows, _ = out.shape
    for g in range(groups):
        out[g] = wide[g * rows : (g + 1) * rows]


def clipped(sums, norms, clip_bound, groups):
    vmem = pl.BlockSpec(memory_space=pltpu.VMEM)
    return pl.pallas_call(
        lambda *refs: clip_body(clip_bound, *refs),
        in_specs=[vmem, vmem],
        out_specs=vmem,
        out_shape=jax.ShapeDtypeStruct((groups, SLOTS // groups, LANES), jnp.float32),
        name="clip",
    )(sums, norms)


def row_moves(shards, groups):
    depth = shards // COLS

    def shifted(value, by):
        pairs = [(z * COLS + x, z * COLS + (x + by) % COLS) for z in range(depth) for x in range(COLS)]
        return lax.ppermute(value, "tm", pairs)

    def swapped(value):
        return lax.ppermute(value, "utt", [(i, i ^ 1) for i in range(groups)])

    return swapped, shifted


def column_rows(own, shards):
    depth = shards // COLS
    return lax.all_to_all(
        jnp.broadcast_to(own[None], (depth,) + own.shape),
        "tm",
        0,
        0,
        axis_index_groups=[[z * COLS + x for z in range(depth)] for x in range(COLS)],
        tiled=True,
    )


def per_device(
    glu_out, cotangent, kernel, conv_bias, out_weight, blocks, last_fill, noise_draws, band_coef
):
    frames, width = glu_out.shape
    blk_count = frames // BLOCK
    shards = lax.axis_size("tm")
    groups = lax.axis_size("utt")
    device = lax.axis_index("tm").astype(jnp.int32)
    core = lax.axis_index("utt").astype(jnp.int32) % 2
    col = device % COLS
    scalars = jnp.concatenate(
        [blocks[0], last_fill[0], jnp.stack([device * blk_count, col, core])]
    )
    swapped, shifted = row_moves(shards, groups)
    half = width // 2
    own = column_rows(lax.dynamic_slice_in_dim(out_weight, core * half, half, axis=1), shards)
    forward = [(i, i + 1) for i in range(shards - 1)]
    backward = [(target, source) for source, target in forward]
    low = lax.ppermute(glu_out[frames - RIM :], "tm", forward)
    high = lax.ppermute(glu_out[:RIM], "tm", backward)
    inner, outer = tuple(range(1, blk_count - 1)), (0, blk_count - 1)
    bias = conv_bias[None]
    hidden_in, *half_in = conv(inner, scalars, glu_out, [], kernel, bias)
    own, hidden_in, low, high = lax.optimization_barrier((own, hidden_in, low, high))
    below, above = shifted(own, 1), shifted(own, -1)
    own_mate = swapped(own)
    hidden_out, *half_out = conv(outer, scalars, glu_out, [low, high], kernel, bias)
    below, above, own_mate, hidden_out = lax.optimization_barrier((below, above, own_mate, hidden_out))
    halves = [(inner, *half_in), (outer, *half_out)]
    mid = shards // COLS // 2
    far_low, far_high = shifted(below[:mid], 1), shifted(above[mid:], -1)
    whole = Rows(
        (own, own_mate), (below, swapped(below)), (above, swapped(above)),
        (far_low, swapped(far_low)), (far_high, swapped(far_high)),
    )
    parts = grads(scalars, cotangent, halves, whole)
    parts = parts.reshape(shards, width // shards, parts.shape[1])
    parts = lax.all_to_all(parts, "tm", 0, 0, tiled=True)
    block_out = project(scalars, [inner, outer], [hidden_in, hidden_out], whole)
    parts, block_out = lax.optimization_barrier((parts, block_out))
    sums, norms = sums_and_norms(scalars, parts)
    norms = lax.all_to_all(norms, "tm", 0, 0, tiled=True)
    clip_bound = 300.0 * math.sqrt(width)
    contrib = clipped(sums, norms, clip_bound, groups)
    contrib = lax.all_to_all(contrib, "utt", 0, 0, tiled=True)
    own_share = jnp.sum(contrib, axis=0)[:, : width // shards]
    mixture = jnp.sum(band_coef[:, None, None] * noise_draws, axis=0)
    mean_grad = (own_share + 0.1 * clip_bound * mixture) / (UTTS * groups)
    return (block_out, mean_grad)


def solution(mesh):
    return jax.shard_map(
        per_device,
        mesh=mesh,
        in_specs=(
            P(("utt", "tm"), None),
            P(("utt", "tm"), None),
            P(),
            P(),
            P("tm", None),
            P("utt", None),
            P("utt", None),
            P(None, "utt", "tm"),
            P(),
        ),
        out_specs=(P(("utt", "tm"), None), P("utt", "tm")),
        check_vma=False,
    )
```

```python
import math

import jax
import jax.numpy as jnp
from jax import lax
from jax.experimental import pallas as pl
from jax.experimental.pallas import tpu as pltpu
from jax.sharding import PartitionSpec as P

BLOCK = 128
LANES = 128
RIM = 16
PADDED = BLOCK + 2 * RIM
STEP = 384
SLOTS = 32
COLS = 4
UTTS = 8
VMEM = 60 << 20


def block_facts(scalars, utts, index):
    utt, limit, cumul = jnp.int32(0), jnp.int32(BLOCK), jnp.int32(0)
    for i in range(utts):
        cumul = cumul + scalars[i]
        utt = utt + (cumul <= index).astype(jnp.int32)
        limit = jnp.where(cumul - 1 == index, scalars[utts + i], limit)
    return utt, limit


def conv_body(blks, scalars, x, *rest):
    rims, (kernel, bias, hidden, slope, padded) = rest[:-5], rest[-5:]
    count = x.shape[0] // BLOCK
    first = scalars[2 * UTTS]
    row = lax.broadcasted_iota(jnp.int32, (BLOCK, LANES), 0)
    rim_row = lax.broadcasted_iota(jnp.int32, (RIM, LANES), 0)
    facts = {}
    for b in blks:
        for near in (b - 1, b, b + 1):
            if near not in facts:
                facts[near] = block_facts(scalars, UTTS, first + near)
    for tile in range(STEP // LANES):
        lanes = slice(tile * LANES, (tile + 1) * LANES)
        for i, b in enumerate(blks):
            utt, limit = facts[b]
            before = (facts[b - 1][0] == utt) & (first + b > 0)
            after = facts[b + 1][0] == utt
            keep = row < limit
            at = b * BLOCK
            left = x[at - RIM : at, lanes] if b else rims[0][:, lanes]
            right = x[at + BLOCK : at + BLOCK + RIM, lanes] if b < count - 1 else rims[1][:, lanes]
            pad = padded.at[tile, i]
            pad[:RIM] = jnp.where(
                rim_row < jnp.where(before, RIM, 0), left.astype(jnp.float32), 0.0
            )
            pad[RIM : RIM + BLOCK] = jnp.where(
                keep, x[at : at + BLOCK, lanes].astype(jnp.float32), 0.0
            )
            pad[RIM + BLOCK :] = jnp.where(
                rim_row < jnp.where(after, facts[b + 1][1], 0), right.astype(jnp.float32), 0.0
            )
            total = jnp.broadcast_to(bias[:, lanes], (BLOCK, LANES))
            for window, taps in windows(pad):
                for q, k in taps:
                    total = total + kernel[k : k + 1, lanes] * window[8 * q : 8 * q + BLOCK]
            logistic = jax.nn.sigmoid(total)
            to = slice(i * BLOCK, (i + 1) * BLOCK)
            hidden[to, lanes] = jnp.where(keep, total * logistic, 0.0).astype(jnp.bfloat16)
            slope[tile, to] = jnp.where(
                keep, logistic * (1.0 + total * (1.0 - logistic)), 0.0
            ).astype(jnp.bfloat16)


def conv(blks, scalars, x, rims, kernel, bias):
    frames, width = x.shape
    own = len(blks) * BLOCK
    column = lambda rows: pl.BlockSpec((rows, STEP), lambda c: (0, c))
    return pl.pallas_call(
        lambda *refs: conv_body(blks, *refs),
        grid=(width // STEP,),
        in_specs=[pl.BlockSpec(memory_space=pltpu.SMEM), column(frames)]
        + [column(RIM)] * len(rims)
        + [column(kernel.shape[0]), column(1)],
        out_specs=[
            column(own),
            pl.BlockSpec((STEP // LANES, own, LANES), lambda c: (c, 0, 0)),
            pl.BlockSpec((STEP // LANES, len(blks), PADDED, LANES), lambda c: (c, 0, 0, 0)),
        ],
        out_shape=[
            jax.ShapeDtypeStruct((own, width), jnp.bfloat16),
            jax.ShapeDtypeStruct((width // LANES, own, LANES), jnp.bfloat16),
            jax.ShapeDtypeStruct((width // LANES, len(blks), PADDED, LANES), jnp.float32),
        ],
        compiler_params=pltpu.CompilerParams(vmem_limit_bytes=VMEM),
        cost_estimate=pl.CostEstimate(
            flops=64 * own * width, bytes_accessed=40 * own * width, transcendentals=own * width
        ),
        name="conv",
    )(scalars, x, *rims, kernel, bias)


class Rows:
    def __init__(self, own, below, above, far_low, far_high):
        self.pieces = [*own, *below, *above, *far_low, *far_high]

    def copies(self, scalars, pieces, weight, sems, part):
        col, core = scalars[2 * UTTS + 1], scalars[2 * UTTS + 2]
        mid, half = pieces[0].shape[0] // 2, pieces[0].shape[2]
        rows = pl.ds(part * mid, mid)
        found = []
        for i in range(2 * COLS):
            piece = pieces[i + 2 * part].at[...] if i >= 6 else pieces[i].at[rows]
            side = 1 - core if i % 2 else core
            shift = (0, COLS - 1, 1, 2)[i // 2]
            found.append(
                pltpu.make_async_copy(
                    piece,
                    weight.at[
                        rows,
                        lax.rem(col + shift, COLS),
                        :,
                        pl.ds(pl.multiple_of(side * half, half), half),
                    ],
                    sems.at[part, i],
                )
            )
        return found

    def scratch(self):
        depth, run, half = self.pieces[0].shape
        return [
            pltpu.VMEM((depth, COLS, run, 2 * half), jnp.bfloat16),
            pltpu.SemaphoreType.DMA((2, 2 * COLS)),
        ]

    def specs(self):
        return [pl.BlockSpec(memory_space=pl.ANY)] * len(self.pieces)


def windows(pad):
    for shift in range(8):
        taps = [(q, 8 * q + shift - 1) for q in range(4) if 0 <= 8 * q + shift - 1 < SLOTS - 1]
        yield pad[shift : shift + BLOCK + 24], taps


def tap_sums(own, pad, b, parts):
    def keep(k, term):
        at = (b * SLOTS + k) * 8
        parts[at : at + 8] = jnp.sum(term.reshape(BLOCK // 8, 8, LANES), axis=0)

    for window, taps in windows(pad):
        for q, k in taps:
            keep(k, own * window[8 * q : 8 * q + BLOCK])
    keep(SLOTS - 1, own)


def grads_body(whole, orders, scalars, cot_far, *rest):
    count = len(orders)
    far, rest = rest[: 2 * count], rest[2 * count :]
    pieces, rest = rest[: len(whole.pieces)], rest[len(whole.pieces) :]
    out, weight, row_sems, cot, *rest = rest
    near, (grad, parts, sems) = rest[: 2 * count], rest[2 * count :]
    depth, cols, run, width = weight.shape
    blks = cot.shape[0] // BLOCK
    steps = 2
    per = depth // steps
    wide_step = per * cols * run
    tiles = wide_step // LANES
    row_copies = [whole.copies(scalars, pieces, weight, row_sems, i) for i in range(steps)]
    head = 3
    first, later = [], []
    for i, (source, target) in enumerate(zip(far, near)):
        for j, (found, low, high) in enumerate(((first, 0, head), (later, head, source.shape[0]))):
            found.append(
                pltpu.make_async_copy(source.at[low:high], target.at[low:high], sems.at[2 * i + j])
            )
    cot_copy = pltpu.make_async_copy(cot_far, cot, sems.at[2 * len(far)])
    for copy in [cot_copy] + row_copies[0]:
        copy.start()

    def taps(step, tile):
        column = step * tiles + tile
        for h, order in enumerate(orders):
            slope, padded = near[2 * h], near[2 * h + 1]
            for i, b in enumerate(order):
                factor = slope[column, i * BLOCK : (i + 1) * BLOCK].astype(jnp.float32)
                tap_sums(grad[tile, b * BLOCK : (b + 1) * BLOCK] * factor, padded.at[column, i], b, parts.at[tile])
        total = parts[tile, pl.ds(0, blks * SLOTS, stride=8)]
        for s in range(1, 8):
            total = total + parts[tile, pl.ds(s, blks * SLOTS, stride=8)]
        out[pl.ds(pl.multiple_of(column * LANES, LANES), LANES)] = total.T.astype(out.dtype)

    def one(step, carry):
        @pl.when(step == 0)
        def _():
            for copy in [cot_copy] + row_copies[0]:
                copy.wait()
            for copy in first + later + row_copies[1]:
                copy.start()

        @pl.when(step == 1)
        def _():
            for copy in row_copies[1]:
                copy.wait()

        hidden_grad = lax.dot_general(
            cot[...],
            weight[pl.ds(step * per, per)].reshape(wide_step, width),
            (((1,), (1,)), ((), ())),
            preferred_element_type=jnp.float32,
        )
        for tile in range(tiles):
            grad[tile] = hidden_grad[:, tile * LANES : (tile + 1) * LANES]

        for low, high, copies in ((0, head, first), (head, tiles, later)):

            @pl.when(step == 0)
            def _():
                for copy in copies:
                    copy.wait()

            for tile in range(low, high):
                taps(step, tile)
        return carry

    lax.fori_loop(0, steps, one, 0)


def grads(scalars, cot, halves, whole):
    frames, width = cot.shape
    blks = frames // BLOCK
    orders = [half[0] for half in halves]
    arrays = [array for half in halves for array in half[1:]]
    anywhere = pl.BlockSpec(memory_space=pl.ANY)
    return pl.pallas_call(
        lambda *refs: grads_body(whole, orders, *refs),
        in_specs=[pl.BlockSpec(memory_space=pltpu.SMEM), anywhere] + [anywhere] * len(arrays) + whole.specs(),
        out_specs=pl.BlockSpec(memory_space=pltpu.VMEM),
        out_shape=jax.ShapeDtypeStruct((width, blks * SLOTS), jnp.bfloat16),
        scratch_shapes=whole.scratch()
        + [pltpu.VMEM(array.shape, array.dtype) for array in [cot] + arrays]
        + [
            pltpu.VMEM((width // 2 // LANES, frames, LANES), jnp.float32),
            pltpu.VMEM((width // 2 // LANES, blks * SLOTS * 8, LANES), jnp.float32),
            pltpu.SemaphoreType.DMA((1 + 2 * len(arrays),)),
        ],
        compiler_params=pltpu.CompilerParams(vmem_limit_bytes=VMEM),
        cost_estimate=pl.CostEstimate(
            flops=2 * frames * width * width, bytes_accessed=20 * frames * width, transcendentals=0
        ),
        name="grads",
    )(scalars, cot, *arrays, *whole.pieces)


def project_body(whole, orders, scalars, *refs):
    hiddens, rest = refs[: len(orders)], refs[len(orders) :]
    pieces, (out, weight, sems) = rest[:-3], rest[-3:]

    @pl.when(pl.program_id(0) == 0)
    def _():
        found = [copy for part in range(2) for copy in whole.copies(scalars, pieces, weight, sems, part)]
        for copy in found:
            copy.start()
        for copy in found:
            copy.wait()

    step = out.shape[1]
    lanes = pl.ds(pl.multiple_of(pl.program_id(0) * step, step), step)
    for order, hidden in zip(orders, hiddens):
        product = jnp.dot(
            hidden[...],
            weight[:, :, :, lanes].reshape(hidden.shape[1], step),
            preferred_element_type=jnp.float32,
        )
        for i, b in enumerate(order):
            out[b * BLOCK : (b + 1) * BLOCK] = product[i * BLOCK : (i + 1) * BLOCK].astype(out.dtype)


def project(scalars, orders, hiddens, whole):
    width = hiddens[0].shape[1]
    frames = sum(hidden.shape[0] for hidden in hiddens)
    step = 512
    return pl.pallas_call(
        lambda *refs: project_body(whole, orders, *refs),
        grid=(width // step,),
        in_specs=[pl.BlockSpec(memory_space=pltpu.SMEM)]
        + [pl.BlockSpec(hidden.shape, lambda c: (0, 0)) for hidden in hiddens]
        + whole.specs(),
        out_specs=pl.BlockSpec((frames, step), lambda c: (0, c)),
        out_shape=jax.ShapeDtypeStruct((frames, width), jnp.bfloat16),
        scratch_shapes=whole.scratch(),
        compiler_params=pltpu.CompilerParams(vmem_limit_bytes=VMEM),
        cost_estimate=pl.CostEstimate(
            flops=2 * frames * width * width, bytes_accessed=2 * width * width + 4 * frames * width, transcendentals=0
        ),
        name="project",
    )(scalars, *hiddens, *whole.pieces)


def sums_body(scalars, parts, norms, *rest):
    outs, (chosen, shares) = rest[:-2], rest[-2:]
    senders, channels, lanes = parts.shape
    groups = len(outs)
    per = lanes // SLOTS
    blk = lax.broadcasted_iota(jnp.int32, (senders, lanes), 0) * per + (
        lax.broadcasted_iota(jnp.int32, (senders, lanes), 1) // SLOTS
    )
    utt_of, cumul = jnp.zeros((senders, lanes), jnp.int32), jnp.int32(0)
    for i in range(UTTS):
        cumul = cumul + scalars[i]
        utt_of = utt_of + (cumul <= blk).astype(jnp.int32)
    for u in range(UTTS):
        chosen[u] = jnp.where(utt_of == u, 1.0, 0.0)
    spot = lax.broadcasted_iota(jnp.int32, (1, lanes), 1)
    row = jnp.zeros((1, lanes), jnp.float32)
    rest = jnp.zeros((lanes - channels, lanes), jnp.float32)
    for few in range(0, UTTS, 4):
        totals = [jnp.zeros((channels, lanes), jnp.float32) for _ in range(4)]
        for s in range(senders):
            part = parts[s].astype(jnp.float32)
            for u in range(4):
                totals[u] = totals[u] + chosen[few + u, s : s + 1] * part
        for u in range(4):
            turned = jnp.concatenate([totals[u], rest], axis=0).T
            total = turned[:SLOTS]
            for i in range(1, per):
                total = total + turned[i * SLOTS : (i + 1) * SLOTS]
            rows = SLOTS // groups
            at = (few + u) * rows
            shares[:, at : at + rows, :] = total.reshape(groups, rows, lanes)
            square = jnp.sum(jnp.sum(total * total, axis=0, keepdims=True), axis=1, keepdims=True)
            row = row + jnp.where(spot == few + u, square, 0.0)
    norms[...] = jnp.broadcast_to(row[None], norms.shape)
    for k, out in enumerate(outs):
        out[...] = shares[scalars[2 * UTTS + 3] ^ k]


def sums_and_norms(scalars, parts, groups):
    senders, channels, lanes = parts.shape
    whole = lambda shape: pl.BlockSpec(shape, lambda c: (0, 0, 0))
    rows = UTTS * SLOTS // groups
    norms = (groups * senders, 1, lanes)
    return pl.pallas_call(
        sums_body,
        grid=(1,),
        in_specs=[pl.BlockSpec(memory_space=pltpu.SMEM), whole(parts.shape)],
        out_specs=[whole(norms)] + [pl.BlockSpec((rows, lanes), lambda c: (0, 0))] * groups,
        out_shape=[jax.ShapeDtypeStruct(norms, jnp.float32)]
        + [jax.ShapeDtypeStruct((rows, lanes), jnp.float32)] * groups,
        scratch_shapes=[
            pltpu.VMEM((UTTS, senders, lanes), jnp.float32),
            pltpu.VMEM((groups, rows, lanes), jnp.float32),
        ],
        compiler_params=pltpu.CompilerParams(vmem_limit_bytes=VMEM),
        name="sums",
    )(scalars, parts)


def finish_body(clip_bound, scalars, coef, norms, draws, *rest):
    shares, out = rest[:-1], rest[-1]
    groups, (rows, lanes) = len(shares), shares[0].shape
    senders = norms.shape[0] // groups
    taps, channels = out.shape
    owner = lax.broadcasted_iota(jnp.int32, (rows, lanes), 0) // taps
    mine = owner == lax.broadcasted_iota(jnp.int32, (rows, lanes), 1)
    total = jnp.zeros((rows, lanes), jnp.float32)
    for k in range(groups):
        start = (scalars[2 * UTTS + 3] ^ k) * senders
        square = jnp.sum(norms[pl.ds(start, senders)], axis=0)
        factor = clip_bound / jnp.maximum(jnp.sqrt(square), clip_bound)
        own = jnp.sum(jnp.where(mine, factor, 0.0), axis=1, keepdims=True)
        total = total + own * shares[k][...]
    clipped = total[:taps]
    for u in range(1, UTTS):
        clipped = clipped + total[u * taps : (u + 1) * taps]
    mixture = coef[0] * draws[0]
    for j in range(1, draws.shape[0]):
        mixture = mixture + coef[j] * draws[j]
    out[...] = (clipped[:, :channels] + 0.1 * clip_bound * mixture) / (UTTS * groups)


def finish(scalars, coef, shares, norms, draws, clip_bound):
    whole = lambda shape: pl.BlockSpec(shape, lambda c: (0,) * len(shape))
    out = draws.shape[1:]
    return pl.pallas_call(
        lambda *refs: finish_body(clip_bound, *refs),
        grid=(1,),
        in_specs=[pl.BlockSpec(memory_space=pltpu.SMEM)] * 2
        + [whole(array.shape) for array in (norms, draws, *shares)],
        out_specs=whole(out),
        out_shape=jax.ShapeDtypeStruct(out, jnp.float32),
        compiler_params=pltpu.CompilerParams(vmem_limit_bytes=VMEM),
        name="finish",
    )(scalars, coef, norms, draws, *shares)


def row_moves(shards, groups):
    depth = shards // COLS

    def shifted(value, by):
        pairs = [(z * COLS + x, z * COLS + (x + by) % COLS) for z in range(depth) for x in range(COLS)]
        return lax.ppermute(value, "tm", pairs)

    def swapped(value):
        return lax.ppermute(value, "utt", [(i, i ^ 1) for i in range(groups)])

    return swapped, shifted


def column_rows(own, shards):
    depth = shards // COLS
    return lax.all_to_all(
        jnp.broadcast_to(own[None], (depth,) + own.shape),
        "tm",
        0,
        0,
        axis_index_groups=[[z * COLS + x for z in range(depth)] for x in range(COLS)],
        tiled=True,
    )


def per_device(
    glu_out, cotangent, kernel, conv_bias, out_weight, blocks, last_fill, noise_draws, band_coef
):
    frames, width = glu_out.shape
    blk_count = frames // BLOCK
    shards = lax.axis_size("tm")
    groups = lax.axis_size("utt")
    device = lax.axis_index("tm").astype(jnp.int32)
    group = lax.axis_index("utt").astype(jnp.int32)
    core = group % 2
    col = device % COLS
    scalars = jnp.concatenate(
        [blocks[0], last_fill[0], jnp.stack([device * blk_count, col, core, group])]
    )
    swapped, shifted = row_moves(shards, groups)
    half = width // 2
    own = column_rows(lax.dynamic_slice_in_dim(out_weight, core * half, half, axis=1), shards)
    forward = [(i, i + 1) for i in range(shards - 1)]
    backward = [(target, source) for source, target in forward]
    low = lax.ppermute(glu_out[frames - RIM :], "tm", forward)
    high = lax.ppermute(glu_out[:RIM], "tm", backward)
    inner, outer = tuple(range(1, blk_count - 1)), (0, blk_count - 1)
    bias = conv_bias[None]
    hidden_in, *half_in = conv(inner, scalars, glu_out, [], kernel, bias)
    own, hidden_in, low, high = lax.optimization_barrier((own, hidden_in, low, high))
    below, above = shifted(own, 1), shifted(own, -1)
    own_mate = swapped(own)
    hidden_out, *half_out = conv(outer, scalars, glu_out, [low, high], kernel, bias)
    below, above, own_mate, hidden_out = lax.optimization_barrier((below, above, own_mate, hidden_out))
    halves = [(inner, *half_in), (outer, *half_out)]
    mid = shards // COLS // 2
    far_low, far_high = shifted(below[:mid], 1), shifted(above[mid:], -1)
    whole = Rows(
        (own, own_mate), (below, swapped(below)), (above, swapped(above)),
        (far_low, swapped(far_low)), (far_high, swapped(far_high)),
    )
    parts = grads(scalars, cotangent, halves, whole)
    parts = parts.reshape(shards, width // shards, parts.shape[1])
    parts = lax.all_to_all(parts, "tm", 0, 0, tiled=True)
    block_out = project(scalars, [inner, outer], [hidden_in, hidden_out], whole)
    parts, block_out = lax.optimization_barrier((parts, block_out))
    norms, *shares = sums_and_norms(scalars, parts, groups)
    norms = lax.all_to_all(norms, ("utt", "tm"), 0, 0, tiled=True)
    shares = shares[:1] + [
        lax.ppermute(shares[k], "utt", [(g, g ^ k) for g in range(groups)]) for k in range(1, groups)
    ]
    mean_grad = finish(scalars, band_coef, shares, norms, noise_draws, 300.0 * math.sqrt(width))
    return (block_out, mean_grad)


def solution(mesh):
    return jax.shard_map(
        per_device,
        mesh=mesh,
        in_specs=(
            P(("utt", "tm"), None),
            P(("utt", "tm"), None),
            P(),
            P(),
            P("tm", None),
            P("utt", None),
            P("utt", None),
            P(None, "utt", "tm"),
            P(),
        ),
        out_specs=(P(("utt", "tm"), None), P("utt", "tm")),
        check_vma=False,
    )
```

```python
import math

import jax
import jax.numpy as jnp
from jax import lax
from jax.experimental import pallas as pl
from jax.experimental.pallas import tpu as pltpu
from jax.sharding import PartitionSpec as P

BLOCK = 128
LANES = 128
RIM = 16
PADDED = BLOCK + 2 * RIM
STEP = 384
SLOTS = 32
COLS = 4
UTTS = 8
VMEM = 60 << 20
SMALL = 8 << 20


def block_facts(scalars, utts, index):
    utt, limit, cumul = jnp.int32(0), jnp.int32(BLOCK), jnp.int32(0)
    for i in range(utts):
        cumul = cumul + scalars[i]
        utt = utt + (cumul <= index).astype(jnp.int32)
        limit = jnp.where(cumul - 1 == index, scalars[utts + i], limit)
    return utt, limit


def conv_body(blks, scalars, x, *rest):
    rims, (kernel, bias, hidden, slope, padded) = rest[:-5], rest[-5:]
    count = x.shape[0] // BLOCK
    first = scalars[2 * UTTS]
    row = lax.broadcasted_iota(jnp.int32, (BLOCK, LANES), 0)
    rim_row = lax.broadcasted_iota(jnp.int32, (RIM, LANES), 0)
    facts = {}
    for b in blks:
        for near in (b - 1, b, b + 1):
            if near not in facts:
                facts[near] = block_facts(scalars, UTTS, first + near)
    for tile in range(STEP // LANES):
        lanes = slice(tile * LANES, (tile + 1) * LANES)
        for i, b in enumerate(blks):
            utt, limit = facts[b]
            before = (facts[b - 1][0] == utt) & (first + b > 0)
            after = facts[b + 1][0] == utt
            keep = row < limit
            at = b * BLOCK
            left = x[at - RIM : at, lanes] if b else rims[0][:, lanes]
            right = x[at + BLOCK : at + BLOCK + RIM, lanes] if b < count - 1 else rims[1][:, lanes]
            pad = padded.at[tile, i]
            pad[:RIM] = jnp.where(
                rim_row < jnp.where(before, RIM, 0), left.astype(jnp.float32), 0.0
            )
            pad[RIM : RIM + BLOCK] = jnp.where(
                keep, x[at : at + BLOCK, lanes].astype(jnp.float32), 0.0
            )
            pad[RIM + BLOCK :] = jnp.where(
                rim_row < jnp.where(after, facts[b + 1][1], 0), right.astype(jnp.float32), 0.0
            )
            total = jnp.broadcast_to(bias[:, lanes], (BLOCK, LANES))
            for window, taps in windows(pad):
                for q, k in taps:
                    total = total + kernel[k : k + 1, lanes] * window[8 * q : 8 * q + BLOCK]
            logistic = jax.nn.sigmoid(total)
            to = slice(i * BLOCK, (i + 1) * BLOCK)
            hidden[to, lanes] = jnp.where(keep, total * logistic, 0.0).astype(jnp.bfloat16)
            slope[tile, to] = jnp.where(
                keep, logistic * (1.0 + total * (1.0 - logistic)), 0.0
            ).astype(jnp.bfloat16)


def conv(blks, scalars, x, rims, kernel, bias):
    frames, width = x.shape
    own = len(blks) * BLOCK
    column = lambda rows: pl.BlockSpec((rows, STEP), lambda c: (0, c))
    return pl.pallas_call(
        lambda *refs: conv_body(blks, *refs),
        grid=(width // STEP,),
        in_specs=[pl.BlockSpec(memory_space=pltpu.SMEM), column(frames)]
        + [column(RIM)] * len(rims)
        + [column(kernel.shape[0]), column(1)],
        out_specs=[
            column(own),
            pl.BlockSpec((STEP // LANES, own, LANES), lambda c: (c, 0, 0)),
            pl.BlockSpec((STEP // LANES, len(blks), PADDED, LANES), lambda c: (c, 0, 0, 0)),
        ],
        out_shape=[
            jax.ShapeDtypeStruct((own, width), jnp.bfloat16),
            jax.ShapeDtypeStruct((width // LANES, own, LANES), jnp.bfloat16),
            jax.ShapeDtypeStruct((width // LANES, len(blks), PADDED, LANES), jnp.float32),
        ],
        compiler_params=pltpu.CompilerParams(vmem_limit_bytes=VMEM),
        cost_estimate=pl.CostEstimate(
            flops=64 * own * width, bytes_accessed=40 * own * width, transcendentals=own * width
        ),
        name="conv",
    )(scalars, x, *rims, kernel, bias)


class Rows:
    def __init__(self, own, below, above, far_low, far_high):
        self.pieces = [*own, *below, *above, *far_low, *far_high]

    def copies(self, scalars, pieces, weight, sems, part):
        col, core = scalars[2 * UTTS + 1], scalars[2 * UTTS + 2]
        mid, half = pieces[0].shape[0] // 2, pieces[0].shape[2]
        rows = pl.ds(part * mid, mid)
        found = []
        for i in range(2 * COLS):
            piece = pieces[i + 2 * part].at[...] if i >= 6 else pieces[i].at[rows]
            side = 1 - core if i % 2 else core
            shift = (0, COLS - 1, 1, 2)[i // 2]
            found.append(
                pltpu.make_async_copy(
                    piece,
                    weight.at[
                        rows,
                        lax.rem(col + shift, COLS),
                        :,
                        pl.ds(pl.multiple_of(side * half, half), half),
                    ],
                    sems.at[part, i],
                )
            )
        return found

    def scratch(self):
        depth, run, half = self.pieces[0].shape
        return [
            pltpu.VMEM((depth, COLS, run, 2 * half), jnp.bfloat16),
            pltpu.SemaphoreType.DMA((2, 2 * COLS)),
        ]

    def specs(self):
        return [pl.BlockSpec(memory_space=pl.ANY)] * len(self.pieces)


def windows(pad):
    for shift in range(8):
        taps = [(q, 8 * q + shift - 1) for q in range(4) if 0 <= 8 * q + shift - 1 < SLOTS - 1]
        yield pad[shift : shift + BLOCK + 24], taps


def tap_sums(own, pad, b, parts):
    def keep(k, term):
        at = (b * SLOTS + k) * 8
        parts[at : at + 8] = jnp.sum(term.reshape(BLOCK // 8, 8, LANES), axis=0)

    for window, taps in windows(pad):
        for q, k in taps:
            keep(k, own * window[8 * q : 8 * q + BLOCK])
    keep(SLOTS - 1, own)


def grads_body(whole, orders, scalars, cot_far, *rest):
    count = len(orders)
    far, rest = rest[: 2 * count], rest[2 * count :]
    pieces, rest = rest[: len(whole.pieces)], rest[len(whole.pieces) :]
    out, weight, row_sems, cot, *rest = rest
    near, (grad, parts, sems) = rest[: 2 * count], rest[2 * count :]
    depth, cols, run, width = weight.shape
    blks = cot.shape[0] // BLOCK
    steps = 2
    per = depth // steps
    wide_step = per * cols * run
    tiles = wide_step // LANES
    row_copies = [whole.copies(scalars, pieces, weight, row_sems, i) for i in range(steps)]
    head = 3
    first, later = [], []
    for i, (source, target) in enumerate(zip(far, near)):
        for j, (found, low, high) in enumerate(((first, 0, head), (later, head, source.shape[0]))):
            found.append(
                pltpu.make_async_copy(source.at[low:high], target.at[low:high], sems.at[2 * i + j])
            )
    cot_copy = pltpu.make_async_copy(cot_far, cot, sems.at[2 * len(far)])
    for copy in [cot_copy] + row_copies[0]:
        copy.start()

    def taps(step, tile):
        column = step * tiles + tile
        for h, order in enumerate(orders):
            slope, padded = near[2 * h], near[2 * h + 1]
            for i, b in enumerate(order):
                factor = slope[column, i * BLOCK : (i + 1) * BLOCK].astype(jnp.float32)
                tap_sums(grad[tile, b * BLOCK : (b + 1) * BLOCK] * factor, padded.at[column, i], b, parts.at[tile])
        total = parts[tile, pl.ds(0, blks * SLOTS, stride=8)]
        for s in range(1, 8):
            total = total + parts[tile, pl.ds(s, blks * SLOTS, stride=8)]
        out[pl.ds(pl.multiple_of(column * LANES, LANES), LANES)] = total.T.astype(out.dtype)

    def one(step, carry):
        @pl.when(step == 0)
        def _():
            for copy in [cot_copy] + row_copies[0]:
                copy.wait()
            for copy in first + later + row_copies[1]:
                copy.start()

        @pl.when(step == 1)
        def _():
            for copy in row_copies[1]:
                copy.wait()

        hidden_grad = lax.dot_general(
            cot[...],
            weight[pl.ds(step * per, per)].reshape(wide_step, width),
            (((1,), (1,)), ((), ())),
            preferred_element_type=jnp.float32,
        )
        for tile in range(tiles):
            grad[tile] = hidden_grad[:, tile * LANES : (tile + 1) * LANES]

        for low, high, copies in ((0, head, first), (head, tiles, later)):

            @pl.when(step == 0)
            def _():
                for copy in copies:
                    copy.wait()

            for tile in range(low, high):
                taps(step, tile)
        return carry

    lax.fori_loop(0, steps, one, 0)


def grads(scalars, cot, halves, whole):
    frames, width = cot.shape
    blks = frames // BLOCK
    orders = [half[0] for half in halves]
    arrays = [array for half in halves for array in half[1:]]
    anywhere = pl.BlockSpec(memory_space=pl.ANY)
    return pl.pallas_call(
        lambda *refs: grads_body(whole, orders, *refs),
        in_specs=[pl.BlockSpec(memory_space=pltpu.SMEM), anywhere] + [anywhere] * len(arrays) + whole.specs(),
        out_specs=pl.BlockSpec(memory_space=pltpu.VMEM),
        out_shape=jax.ShapeDtypeStruct((width, blks * SLOTS), jnp.bfloat16),
        scratch_shapes=whole.scratch()
        + [pltpu.VMEM(array.shape, array.dtype) for array in [cot] + arrays]
        + [
            pltpu.VMEM((width // 2 // LANES, frames, LANES), jnp.float32),
            pltpu.VMEM((width // 2 // LANES, blks * SLOTS * 8, LANES), jnp.float32),
            pltpu.SemaphoreType.DMA((1 + 2 * len(arrays),)),
        ],
        compiler_params=pltpu.CompilerParams(vmem_limit_bytes=VMEM),
        cost_estimate=pl.CostEstimate(
            flops=2 * frames * width * width, bytes_accessed=20 * frames * width, transcendentals=0
        ),
        name="grads",
    )(scalars, cot, *arrays, *whole.pieces)


def project_body(whole, orders, scalars, *refs):
    hiddens, rest = refs[: len(orders)], refs[len(orders) :]
    pieces, (out, weight, sems) = rest[:-3], rest[-3:]

    @pl.when(pl.program_id(0) == 0)
    def _():
        found = [copy for part in range(2) for copy in whole.copies(scalars, pieces, weight, sems, part)]
        for copy in found:
            copy.start()
        for copy in found:
            copy.wait()

    step = out.shape[1]
    lanes = pl.ds(pl.multiple_of(pl.program_id(0) * step, step), step)
    for order, hidden in zip(orders, hiddens):
        product = jnp.dot(
            hidden[...],
            weight[:, :, :, lanes].reshape(hidden.shape[1], step),
            preferred_element_type=jnp.float32,
        )
        for i, b in enumerate(order):
            out[b * BLOCK : (b + 1) * BLOCK] = product[i * BLOCK : (i + 1) * BLOCK].astype(out.dtype)


def project(scalars, orders, hiddens, whole):
    width = hiddens[0].shape[1]
    frames = sum(hidden.shape[0] for hidden in hiddens)
    step = 512
    return pl.pallas_call(
        lambda *refs: project_body(whole, orders, *refs),
        grid=(width // step,),
        in_specs=[pl.BlockSpec(memory_space=pltpu.SMEM)]
        + [pl.BlockSpec(hidden.shape, lambda c: (0, 0)) for hidden in hiddens]
        + whole.specs(),
        out_specs=pl.BlockSpec((frames, step), lambda c: (0, c)),
        out_shape=jax.ShapeDtypeStruct((frames, width), jnp.bfloat16),
        scratch_shapes=whole.scratch(),
        compiler_params=pltpu.CompilerParams(vmem_limit_bytes=VMEM),
        cost_estimate=pl.CostEstimate(
            flops=2 * frames * width * width, bytes_accessed=2 * width * width + 4 * frames * width, transcendentals=0
        ),
        name="project",
    )(scalars, *hiddens, *whole.pieces)


def sums_body(scalars, parts, norms, *rest):
    outs, (chosen, shares) = rest[:-2], rest[-2:]
    senders, channels, lanes = parts.shape
    groups = len(outs)
    per = lanes // SLOTS
    blk = lax.broadcasted_iota(jnp.int32, (senders, lanes), 0) * per + (
        lax.broadcasted_iota(jnp.int32, (senders, lanes), 1) // SLOTS
    )
    utt_of, cumul = jnp.zeros((senders, lanes), jnp.int32), jnp.int32(0)
    for i in range(UTTS):
        cumul = cumul + scalars[i]
        utt_of = utt_of + (cumul <= blk).astype(jnp.int32)
    for u in range(UTTS):
        chosen[u] = jnp.where(utt_of == u, 1.0, 0.0)
    spot = lax.broadcasted_iota(jnp.int32, (1, lanes), 1)
    row = jnp.zeros((1, lanes), jnp.float32)
    rest = jnp.zeros((lanes - channels, lanes), jnp.float32)
    for few in range(0, UTTS, 4):
        totals = [jnp.zeros((channels, lanes), jnp.float32) for _ in range(4)]
        for s in range(senders):
            part = parts[s].astype(jnp.float32)
            for u in range(4):
                totals[u] = totals[u] + chosen[few + u, s : s + 1] * part
        for u in range(4):
            turned = jnp.concatenate([totals[u], rest], axis=0).T
            total = turned[:SLOTS]
            for i in range(1, per):
                total = total + turned[i * SLOTS : (i + 1) * SLOTS]
            rows = SLOTS // groups
            at = (few + u) * rows
            shares[:, at : at + rows, :] = total.reshape(groups, rows, lanes)
            square = jnp.sum(jnp.sum(total * total, axis=0, keepdims=True), axis=1, keepdims=True)
            row = row + jnp.where(spot == few + u, square, 0.0)
    norms[...] = jnp.broadcast_to(row[None], norms.shape)
    for k, out in enumerate(outs):
        out[...] = shares[scalars[2 * UTTS + 3] ^ k]


def sums_and_norms(scalars, parts, groups):
    senders, channels, lanes = parts.shape
    whole = lambda shape: pl.BlockSpec(shape, lambda c: (0, 0, 0))
    rows = UTTS * SLOTS // groups
    norms = (groups * senders, 1, lanes)
    return pl.pallas_call(
        sums_body,
        grid=(1,),
        in_specs=[pl.BlockSpec(memory_space=pltpu.SMEM), whole(parts.shape)],
        out_specs=[whole(norms)] + [pl.BlockSpec((rows, lanes), lambda c: (0, 0))] * groups,
        out_shape=[jax.ShapeDtypeStruct(norms, jnp.float32)]
        + [jax.ShapeDtypeStruct((rows, lanes), jnp.float32)] * groups,
        scratch_shapes=[
            pltpu.VMEM((UTTS, senders, lanes), jnp.float32),
            pltpu.VMEM((groups, rows, lanes), jnp.float32),
        ],
        compiler_params=pltpu.CompilerParams(vmem_limit_bytes=SMALL),
        name="sums",
    )(scalars, parts)


def finish_body(clip_bound, scalars, coef, norms, draws, *rest):
    shares, out = rest[:-1], rest[-1]
    groups, (rows, lanes) = len(shares), shares[0].shape
    senders = norms.shape[0] // groups
    taps, channels = out.shape
    owner = lax.broadcasted_iota(jnp.int32, (rows, lanes), 0) // taps
    mine = owner == lax.broadcasted_iota(jnp.int32, (rows, lanes), 1)
    total = jnp.zeros((rows, lanes), jnp.float32)
    for k in range(groups):
        start = (scalars[2 * UTTS + 3] ^ k) * senders
        square = jnp.sum(norms[pl.ds(start, senders)], axis=0)
        factor = clip_bound / jnp.maximum(jnp.sqrt(square), clip_bound)
        own = jnp.sum(jnp.where(mine, factor, 0.0), axis=1, keepdims=True)
        total = total + own * shares[k][...]
    clipped = total[:taps]
    for u in range(1, UTTS):
        clipped = clipped + total[u * taps : (u + 1) * taps]
    mixture = coef[0] * draws[0]
    for j in range(1, draws.shape[0]):
        mixture = mixture + coef[j] * draws[j]
    out[...] = (clipped[:, :channels] + 0.1 * clip_bound * mixture) / (UTTS * groups)


def finish(scalars, coef, shares, norms, draws, clip_bound):
    whole = lambda shape: pl.BlockSpec(shape, lambda c: (0,) * len(shape))
    out = draws.shape[1:]
    return pl.pallas_call(
        lambda *refs: finish_body(clip_bound, *refs),
        grid=(1,),
        in_specs=[pl.BlockSpec(memory_space=pltpu.SMEM)] * 2
        + [whole(array.shape) for array in (norms, draws, *shares)],
        out_specs=whole(out),
        out_shape=jax.ShapeDtypeStruct(out, jnp.float32),
        compiler_params=pltpu.CompilerParams(vmem_limit_bytes=SMALL),
        name="finish",
    )(scalars, coef, norms, draws, *shares)


def row_moves(shards, groups):
    depth = shards // COLS

    def shifted(value, by):
        pairs = [(z * COLS + x, z * COLS + (x + by) % COLS) for z in range(depth) for x in range(COLS)]
        return lax.ppermute(value, "tm", pairs)

    def swapped(value):
        return lax.ppermute(value, "utt", [(i, i ^ 1) for i in range(groups)])

    return swapped, shifted


def spread_body(start, rows, out):
    half = out.shape[2]
    own = rows[:, pl.ds(pl.multiple_of(start[0], half), half)]
    for z in range(out.shape[0]):
        out[z] = own


def column_rows(out_weight, core, shards):
    depth = shards // COLS
    run, half = out_weight.shape[0], out_weight.shape[1] // 2
    copies = pl.pallas_call(
        spread_body,
        grid=(1,),
        in_specs=[
            pl.BlockSpec(memory_space=pltpu.SMEM),
            pl.BlockSpec((run, out_weight.shape[1]), lambda c: (0, 0)),
        ],
        out_specs=pl.BlockSpec((depth, run, half), lambda c: (0, 0, 0)),
        out_shape=jax.ShapeDtypeStruct((depth, run, half), out_weight.dtype),
        compiler_params=pltpu.CompilerParams(vmem_limit_bytes=VMEM),
        name="spread",
    )((core * half).reshape(1), out_weight)
    return lax.all_to_all(
        copies,
        "tm",
        0,
        0,
        axis_index_groups=[[z * COLS + x for z in range(depth)] for x in range(COLS)],
        tiled=True,
    )


def per_device(
    glu_out, cotangent, kernel, conv_bias, out_weight, blocks, last_fill, noise_draws, band_coef
):
    frames, width = glu_out.shape
    blk_count = frames // BLOCK
    shards = lax.axis_size("tm")
    groups = lax.axis_size("utt")
    device = lax.axis_index("tm").astype(jnp.int32)
    group = lax.axis_index("utt").astype(jnp.int32)
    core = group % 2
    col = device % COLS
    scalars = jnp.concatenate(
        [blocks[0], last_fill[0], jnp.stack([device * blk_count, col, core, group])]
    )
    swapped, shifted = row_moves(shards, groups)
    own = column_rows(out_weight, core, shards)
    forward = [(i, i + 1) for i in range(shards - 1)]
    backward = [(target, source) for source, target in forward]
    low = lax.ppermute(glu_out[frames - RIM :], "tm", forward)
    high = lax.ppermute(glu_out[:RIM], "tm", backward)
    inner, outer = tuple(range(1, blk_count - 1)), (0, blk_count - 1)
    bias = conv_bias[None]
    hidden_in, *half_in = conv(inner, scalars, glu_out, [], kernel, bias)
    own, hidden_in, low, high = lax.optimization_barrier((own, hidden_in, low, high))
    below, above = shifted(own, 1), shifted(own, -1)
    hidden_out, *half_out = conv(outer, scalars, glu_out, [low, high], kernel, bias)
    own, below, above, hidden_out = lax.optimization_barrier((own, below, above, hidden_out))
    own_mate = swapped(own)
    halves = [(inner, *half_in), (outer, *half_out)]
    mid = shards // COLS // 2
    far_low, far_high = shifted(below[:mid], 1), shifted(above[mid:], -1)
    whole = Rows(
        (own, own_mate), (below, swapped(below)), (above, swapped(above)),
        (far_low, swapped(far_low)), (far_high, swapped(far_high)),
    )
    parts = grads(scalars, cotangent, halves, whole)
    parts = parts.reshape(shards, width // shards, parts.shape[1])
    parts = lax.all_to_all(parts, "tm", 0, 0, tiled=True)
    block_out = project(scalars, [inner, outer], [hidden_in, hidden_out], whole)
    parts, block_out = lax.optimization_barrier((parts, block_out))
    norms, *shares = sums_and_norms(scalars, parts, groups)
    norms = lax.all_to_all(norms, ("utt", "tm"), 0, 0, tiled=True)
    shares = shares[:1] + [
        lax.ppermute(shares[k], "utt", [(g, g ^ k) for g in range(groups)]) for k in range(1, groups)
    ]
    mean_grad = finish(scalars, band_coef, shares, norms, noise_draws, 300.0 * math.sqrt(width))
    return (block_out, mean_grad)


def solution(mesh):
    return jax.shard_map(
        per_device,
        mesh=mesh,
        in_specs=(
            P(("utt", "tm"), None),
            P(("utt", "tm"), None),
            P(),
            P(),
            P("tm", None),
            P("utt", None),
            P("utt", None),
            P(None, "utt", "tm"),
            P(),
        ),
        out_specs=(P(("utt", "tm"), None), P("utt", "tm")),
        check_vma=False,
    )
```

```python
import math

import jax
import jax.numpy as jnp
from jax import lax
from jax.experimental import pallas as pl
from jax.experimental.pallas import tpu as pltpu
from jax.sharding import PartitionSpec as P

BLOCK = 128
LANES = 128
RIM = 16
PADDED = BLOCK + 2 * RIM
STEP = 384
SLOTS = 32
COLS = 4
UTTS = 8
VMEM = 52 << 20
SMALL = 8 << 20


def block_facts(scalars, utts, index):
    utt, limit, cumul = jnp.int32(0), jnp.int32(BLOCK), jnp.int32(0)
    for i in range(utts):
        cumul = cumul + scalars[i]
        utt = utt + (cumul <= index).astype(jnp.int32)
        limit = jnp.where(cumul - 1 == index, scalars[utts + i], limit)
    return utt, limit


def conv_body(blks, scalars, x, *rest):
    rims, (kernel, bias, hidden, slope, padded) = rest[:-5], rest[-5:]
    count = x.shape[0] // BLOCK
    first = scalars[2 * UTTS]
    row = lax.broadcasted_iota(jnp.int32, (BLOCK, LANES), 0)
    rim_row = lax.broadcasted_iota(jnp.int32, (RIM, LANES), 0)
    facts = {}
    for b in blks:
        for near in (b - 1, b, b + 1):
            if near not in facts:
                facts[near] = block_facts(scalars, UTTS, first + near)
    for tile in range(STEP // LANES):
        lanes = slice(tile * LANES, (tile + 1) * LANES)
        for i, b in enumerate(blks):
            utt, limit = facts[b]
            before = (facts[b - 1][0] == utt) & (first + b > 0)
            after = facts[b + 1][0] == utt
            keep = row < limit
            at = b * BLOCK
            left = x[at - RIM : at, lanes] if b else rims[0][:, lanes]
            right = x[at + BLOCK : at + BLOCK + RIM, lanes] if b < count - 1 else rims[1][:, lanes]
            pad = padded.at[tile, i]
            pad[:RIM] = jnp.where(
                rim_row < jnp.where(before, RIM, 0), left.astype(jnp.float32), 0.0
            )
            pad[RIM : RIM + BLOCK] = jnp.where(
                keep, x[at : at + BLOCK, lanes].astype(jnp.float32), 0.0
            )
            pad[RIM + BLOCK :] = jnp.where(
                rim_row < jnp.where(after, facts[b + 1][1], 0), right.astype(jnp.float32), 0.0
            )
            total = jnp.broadcast_to(bias[:, lanes], (BLOCK, LANES))
            for window, taps in windows(pad):
                for q, k in taps:
                    total = total + kernel[k : k + 1, lanes] * window[8 * q : 8 * q + BLOCK]
            logistic = jax.nn.sigmoid(total)
            to = slice(i * BLOCK, (i + 1) * BLOCK)
            hidden[to, lanes] = jnp.where(keep, total * logistic, 0.0).astype(jnp.bfloat16)
            slope[tile, to] = jnp.where(
                keep, logistic * (1.0 + total * (1.0 - logistic)), 0.0
            ).astype(jnp.bfloat16)


def conv(blks, scalars, x, rims, kernel, bias):
    frames, width = x.shape
    own = len(blks) * BLOCK
    column = lambda rows: pl.BlockSpec((rows, STEP), lambda c: (0, c))
    return pl.pallas_call(
        lambda *refs: conv_body(blks, *refs),
        grid=(width // STEP,),
        in_specs=[pl.BlockSpec(memory_space=pltpu.SMEM), column(frames)]
        + [column(RIM)] * len(rims)
        + [column(kernel.shape[0]), column(1)],
        out_specs=[
            column(own),
            pl.BlockSpec((STEP // LANES, own, LANES), lambda c: (c, 0, 0)),
            pl.BlockSpec((STEP // LANES, len(blks), PADDED, LANES), lambda c: (c, 0, 0, 0)),
        ],
        out_shape=[
            jax.ShapeDtypeStruct((own, width), jnp.bfloat16),
            jax.ShapeDtypeStruct((width // LANES, own, LANES), jnp.bfloat16),
            jax.ShapeDtypeStruct((width // LANES, len(blks), PADDED, LANES), jnp.float32),
        ],
        compiler_params=pltpu.CompilerParams(vmem_limit_bytes=VMEM),
        cost_estimate=pl.CostEstimate(
            flops=64 * own * width, bytes_accessed=40 * own * width, transcendentals=own * width
        ),
        name="conv",
    )(scalars, x, *rims, kernel, bias)


class Rows:
    def __init__(self, own, below, above, far_low, far_high):
        self.pieces = [*own, *below, *above, *far_low, *far_high]

    def copies(self, scalars, pieces, weight, sems, part):
        col, core = scalars[2 * UTTS + 1], scalars[2 * UTTS + 2]
        mid, half = pieces[0].shape[0] // 2, pieces[0].shape[2]
        rows = pl.ds(part * mid, mid)
        found = []
        for i in range(2 * COLS):
            piece = pieces[i + 2 * part].at[...] if i >= 6 else pieces[i].at[rows]
            side = 1 - core if i % 2 else core
            shift = (0, COLS - 1, 1, 2)[i // 2]
            found.append(
                pltpu.make_async_copy(
                    piece,
                    weight.at[
                        rows,
                        lax.rem(col + shift, COLS),
                        :,
                        pl.ds(pl.multiple_of(side * half, half), half),
                    ],
                    sems.at[part, i],
                )
            )
        return found

    def scratch(self):
        depth, run, half = self.pieces[0].shape
        return [
            pltpu.VMEM((depth, COLS, run, 2 * half), jnp.bfloat16),
            pltpu.SemaphoreType.DMA((2, 2 * COLS)),
        ]

    def specs(self):
        return [pl.BlockSpec(memory_space=pl.ANY)] * len(self.pieces)


def windows(pad):
    for shift in range(8):
        taps = [(q, 8 * q + shift - 1) for q in range(4) if 0 <= 8 * q + shift - 1 < SLOTS - 1]
        yield pad[shift : shift + BLOCK + 24], taps


def tap_sums(own, pad, b, parts):
    def keep(k, term):
        at = (b * SLOTS + k) * 8
        parts[at : at + 8] = jnp.sum(term.reshape(BLOCK // 8, 8, LANES), axis=0)

    for window, taps in windows(pad):
        for q, k in taps:
            keep(k, own * window[8 * q : 8 * q + BLOCK])
    keep(SLOTS - 1, own)


def grads_body(whole, orders, scalars, cot_far, *rest):
    count = len(orders)
    far, rest = rest[: 2 * count], rest[2 * count :]
    pieces, rest = rest[: len(whole.pieces)], rest[len(whole.pieces) :]
    out, weight, row_sems, cot, *rest = rest
    near, (grad, parts, sems) = rest[: 2 * count], rest[2 * count :]
    depth, cols, run, width = weight.shape
    blks = cot.shape[0] // BLOCK
    steps = 2
    per = depth // steps
    wide_step = per * cols * run
    tiles = wide_step // LANES
    row_copies = [whole.copies(scalars, pieces, weight, row_sems, i) for i in range(steps)]
    head = 3
    first, later = [], []
    for i, (source, target) in enumerate(zip(far, near)):
        for j, (found, low, high) in enumerate(((first, 0, head), (later, head, source.shape[0]))):
            found.append(
                pltpu.make_async_copy(source.at[low:high], target.at[low:high], sems.at[2 * i + j])
            )
    cot_copy = pltpu.make_async_copy(cot_far, cot, sems.at[2 * len(far)])
    for copy in [cot_copy] + row_copies[0]:
        copy.start()

    def taps(step, tile):
        column = step * tiles + tile
        for h, order in enumerate(orders):
            slope, padded = near[2 * h], near[2 * h + 1]
            for i, b in enumerate(order):
                factor = slope[column, i * BLOCK : (i + 1) * BLOCK].astype(jnp.float32)
                tap_sums(grad[tile, b * BLOCK : (b + 1) * BLOCK] * factor, padded.at[column, i], b, parts.at[tile])
        total = parts[tile, pl.ds(0, blks * SLOTS, stride=8)]
        for s in range(1, 8):
            total = total + parts[tile, pl.ds(s, blks * SLOTS, stride=8)]
        out[pl.ds(pl.multiple_of(column * LANES, LANES), LANES)] = total.T.astype(out.dtype)

    def one(step, carry):
        @pl.when(step == 0)
        def _():
            for copy in [cot_copy] + row_copies[0]:
                copy.wait()
            for copy in first + later + row_copies[1]:
                copy.start()

        @pl.when(step == 1)
        def _():
            for copy in row_copies[1]:
                copy.wait()

        hidden_grad = lax.dot_general(
            cot[...],
            weight[pl.ds(step * per, per)].reshape(wide_step, width),
            (((1,), (1,)), ((), ())),
            preferred_element_type=jnp.float32,
        )
        for tile in range(tiles):
            grad[tile] = hidden_grad[:, tile * LANES : (tile + 1) * LANES]

        for low, high, copies in ((0, head, first), (head, tiles, later)):

            @pl.when(step == 0)
            def _():
                for copy in copies:
                    copy.wait()

            for tile in range(low, high):
                taps(step, tile)
        return carry

    lax.fori_loop(0, steps, one, 0)


def grads(scalars, cot, halves, whole):
    frames, width = cot.shape
    blks = frames // BLOCK
    orders = [half[0] for half in halves]
    arrays = [array for half in halves for array in half[1:]]
    anywhere = pl.BlockSpec(memory_space=pl.ANY)
    return pl.pallas_call(
        lambda *refs: grads_body(whole, orders, *refs),
        in_specs=[pl.BlockSpec(memory_space=pltpu.SMEM), anywhere] + [anywhere] * len(arrays) + whole.specs(),
        out_specs=pl.BlockSpec(memory_space=pltpu.VMEM),
        out_shape=jax.ShapeDtypeStruct((width, blks * SLOTS), jnp.bfloat16),
        scratch_shapes=whole.scratch()
        + [pltpu.VMEM(array.shape, array.dtype) for array in [cot] + arrays]
        + [
            pltpu.VMEM((width // 2 // LANES, frames, LANES), jnp.float32),
            pltpu.VMEM((width // 2 // LANES, blks * SLOTS * 8, LANES), jnp.float32),
            pltpu.SemaphoreType.DMA((1 + 2 * len(arrays),)),
        ],
        compiler_params=pltpu.CompilerParams(vmem_limit_bytes=VMEM),
        cost_estimate=pl.CostEstimate(
            flops=2 * frames * width * width, bytes_accessed=20 * frames * width, transcendentals=0
        ),
        name="grads",
    )(scalars, cot, *arrays, *whole.pieces)


def project_body(whole, orders, scalars, *refs):
    hiddens, rest = refs[: len(orders)], refs[len(orders) :]
    pieces, (out, weight, sems) = rest[:-3], rest[-3:]

    @pl.when(pl.program_id(0) == 0)
    def _():
        found = [copy for part in range(2) for copy in whole.copies(scalars, pieces, weight, sems, part)]
        for copy in found:
            copy.start()
        for copy in found:
            copy.wait()

    step = out.shape[1]
    lanes = pl.ds(pl.multiple_of(pl.program_id(0) * step, step), step)
    for order, hidden in zip(orders, hiddens):
        product = jnp.dot(
            hidden[...],
            weight[:, :, :, lanes].reshape(hidden.shape[1], step),
            preferred_element_type=jnp.float32,
        )
        for i, b in enumerate(order):
            out[b * BLOCK : (b + 1) * BLOCK] = product[i * BLOCK : (i + 1) * BLOCK].astype(out.dtype)


def project(scalars, orders, hiddens, whole):
    width = hiddens[0].shape[1]
    frames = sum(hidden.shape[0] for hidden in hiddens)
    step = 512
    return pl.pallas_call(
        lambda *refs: project_body(whole, orders, *refs),
        grid=(width // step,),
        in_specs=[pl.BlockSpec(memory_space=pltpu.SMEM)]
        + [pl.BlockSpec(hidden.shape, lambda c: (0, 0)) for hidden in hiddens]
        + whole.specs(),
        out_specs=pl.BlockSpec((frames, step), lambda c: (0, c)),
        out_shape=jax.ShapeDtypeStruct((frames, width), jnp.bfloat16),
        scratch_shapes=whole.scratch(),
        compiler_params=pltpu.CompilerParams(vmem_limit_bytes=VMEM),
        cost_estimate=pl.CostEstimate(
            flops=2 * frames * width * width, bytes_accessed=2 * width * width + 4 * frames * width, transcendentals=0
        ),
        name="project",
    )(scalars, *hiddens, *whole.pieces)


def sums_body(scalars, parts, norms, *rest):
    outs, (chosen, shares) = rest[:-2], rest[-2:]
    senders, channels, lanes = parts.shape
    groups = len(outs)
    per = lanes // SLOTS
    blk = lax.broadcasted_iota(jnp.int32, (senders, lanes), 0) * per + (
        lax.broadcasted_iota(jnp.int32, (senders, lanes), 1) // SLOTS
    )
    utt_of, cumul = jnp.zeros((senders, lanes), jnp.int32), jnp.int32(0)
    for i in range(UTTS):
        cumul = cumul + scalars[i]
        utt_of = utt_of + (cumul <= blk).astype(jnp.int32)
    for u in range(UTTS):
        chosen[u] = jnp.where(utt_of == u, 1.0, 0.0)
    spot = lax.broadcasted_iota(jnp.int32, (1, lanes), 1)
    row = jnp.zeros((1, lanes), jnp.float32)
    rest = jnp.zeros((lanes - channels, lanes), jnp.float32)
    for few in range(0, UTTS, 4):
        totals = [jnp.zeros((channels, lanes), jnp.float32) for _ in range(4)]
        for s in range(senders):
            part = parts[s].astype(jnp.float32)
            for u in range(4):
                totals[u] = totals[u] + chosen[few + u, s : s + 1] * part
        for u in range(4):
            turned = jnp.concatenate([totals[u], rest], axis=0).T
            total = turned[:SLOTS]
            for i in range(1, per):
                total = total + turned[i * SLOTS : (i + 1) * SLOTS]
            rows = SLOTS // groups
            at = (few + u) * rows
            shares[:, at : at + rows, :] = total.reshape(groups, rows, lanes)
            square = jnp.sum(jnp.sum(total * total, axis=0, keepdims=True), axis=1, keepdims=True)
            row = row + jnp.where(spot == few + u, square, 0.0)
    norms[...] = jnp.broadcast_to(row[None], norms.shape)
    for k, out in enumerate(outs):
        out[...] = shares[scalars[2 * UTTS + 3] ^ k]


def sums_and_norms(scalars, parts, groups):
    senders, channels, lanes = parts.shape
    whole = lambda shape: pl.BlockSpec(shape, lambda c: (0, 0, 0))
    rows = UTTS * SLOTS // groups
    norms = (groups * senders, 1, lanes)
    return pl.pallas_call(
        sums_body,
        grid=(1,),
        in_specs=[pl.BlockSpec(memory_space=pltpu.SMEM), whole(parts.shape)],
        out_specs=[whole(norms)] + [pl.BlockSpec((rows, lanes), lambda c: (0, 0))] * groups,
        out_shape=[jax.ShapeDtypeStruct(norms, jnp.float32)]
        + [jax.ShapeDtypeStruct((rows, lanes), jnp.float32)] * groups,
        scratch_shapes=[
            pltpu.VMEM((UTTS, senders, lanes), jnp.float32),
            pltpu.VMEM((groups, rows, lanes), jnp.float32),
        ],
        compiler_params=pltpu.CompilerParams(vmem_limit_bytes=SMALL),
        name="sums",
    )(scalars, parts)


def finish_body(clip_bound, scalars, coef, norms, draws, *rest):
    shares, out = rest[:-1], rest[-1]
    groups, (rows, lanes) = len(shares), shares[0].shape
    senders = norms.shape[0] // groups
    taps, channels = out.shape
    owner = lax.broadcasted_iota(jnp.int32, (rows, lanes), 0) // taps
    mine = owner == lax.broadcasted_iota(jnp.int32, (rows, lanes), 1)
    total = jnp.zeros((rows, lanes), jnp.float32)
    for k in range(groups):
        start = (scalars[2 * UTTS + 3] ^ k) * senders
        square = jnp.sum(norms[pl.ds(start, senders)], axis=0)
        factor = clip_bound / jnp.maximum(jnp.sqrt(square), clip_bound)
        own = jnp.sum(jnp.where(mine, factor, 0.0), axis=1, keepdims=True)
        total = total + own * shares[k][...]
    clipped = total[:taps]
    for u in range(1, UTTS):
        clipped = clipped + total[u * taps : (u + 1) * taps]
    mixture = coef[0] * draws[0]
    for j in range(1, draws.shape[0]):
        mixture = mixture + coef[j] * draws[j]
    out[...] = (clipped[:, :channels] + 0.1 * clip_bound * mixture) / (UTTS * groups)


def finish(scalars, coef, shares, norms, draws, clip_bound):
    whole = lambda shape: pl.BlockSpec(shape, lambda c: (0,) * len(shape))
    out = draws.shape[1:]
    return pl.pallas_call(
        lambda *refs: finish_body(clip_bound, *refs),
        grid=(1,),
        in_specs=[pl.BlockSpec(memory_space=pltpu.SMEM)] * 2
        + [whole(array.shape) for array in (norms, draws, *shares)],
        out_specs=whole(out),
        out_shape=jax.ShapeDtypeStruct(out, jnp.float32),
        compiler_params=pltpu.CompilerParams(vmem_limit_bytes=SMALL),
        name="finish",
    )(scalars, coef, norms, draws, *shares)


def row_moves(shards, groups):
    depth = shards // COLS

    def shifted(value, by):
        pairs = [(z * COLS + x, z * COLS + (x + by) % COLS) for z in range(depth) for x in range(COLS)]
        return lax.ppermute(value, "tm", pairs)

    def swapped(value):
        return lax.ppermute(value, "utt", [(i, i ^ 1) for i in range(groups)])

    return swapped, shifted


def spread_body(start, rows, out):
    half = out.shape[2]
    own = rows[:, pl.ds(pl.multiple_of(start[0], half), half)]
    for z in range(out.shape[0]):
        out[z] = own


def column_rows(out_weight, core, shards):
    depth = shards // COLS
    run, half = out_weight.shape[0], out_weight.shape[1] // 2
    copies = pl.pallas_call(
        spread_body,
        grid=(1,),
        in_specs=[
            pl.BlockSpec(memory_space=pltpu.SMEM),
            pl.BlockSpec((run, out_weight.shape[1]), lambda c: (0, 0)),
        ],
        out_specs=pl.BlockSpec((depth, run, half), lambda c: (0, 0, 0)),
        out_shape=jax.ShapeDtypeStruct((depth, run, half), out_weight.dtype),
        compiler_params=pltpu.CompilerParams(vmem_limit_bytes=VMEM),
        name="spread",
    )((core * half).reshape(1), out_weight)
    return lax.all_to_all(
        copies,
        "tm",
        0,
        0,
        axis_index_groups=[[z * COLS + x for z in range(depth)] for x in range(COLS)],
        tiled=True,
    )


def per_device(
    glu_out, cotangent, kernel, conv_bias, out_weight, blocks, last_fill, noise_draws, band_coef
):
    frames, width = glu_out.shape
    blk_count = frames // BLOCK
    shards = lax.axis_size("tm")
    groups = lax.axis_size("utt")
    device = lax.axis_index("tm").astype(jnp.int32)
    group = lax.axis_index("utt").astype(jnp.int32)
    core = group % 2
    col = device % COLS
    scalars = jnp.concatenate(
        [blocks[0], last_fill[0], jnp.stack([device * blk_count, col, core, group])]
    )
    swapped, shifted = row_moves(shards, groups)
    own = column_rows(out_weight, core, shards)
    forward = [(i, i + 1) for i in range(shards - 1)]
    backward = [(target, source) for source, target in forward]
    low = lax.ppermute(glu_out[frames - RIM :], "tm", forward)
    high = lax.ppermute(glu_out[:RIM], "tm", backward)
    inner, outer = tuple(range(1, blk_count - 1)), (0, blk_count - 1)
    bias = conv_bias[None]
    hidden_in, *half_in = conv(inner, scalars, glu_out, [], kernel, bias)
    own, hidden_in, low, high = lax.optimization_barrier((own, hidden_in, low, high))
    below, above = shifted(own, 1), shifted(own, -1)
    hidden_out, *half_out = conv(outer, scalars, glu_out, [low, high], kernel, bias)
    own, below, above, hidden_out = lax.optimization_barrier((own, below, above, hidden_out))
    own_mate = swapped(own)
    halves = [(inner, *half_in), (outer, *half_out)]
    mid = shards // COLS // 2
    far_low, far_high = shifted(below[:mid], 1), shifted(above[mid:], -1)
    whole = Rows(
        (own, own_mate), (below, swapped(below)), (above, swapped(above)),
        (far_low, swapped(far_low)), (far_high, swapped(far_high)),
    )
    parts = grads(scalars, cotangent, halves, whole)
    parts = parts.reshape(shards, width // shards, parts.shape[1])
    parts = lax.all_to_all(parts, "tm", 0, 0, tiled=True)
    block_out = project(scalars, [inner, outer], [hidden_in, hidden_out], whole)
    parts, block_out = lax.optimization_barrier((parts, block_out))
    norms, *shares = sums_and_norms(scalars, parts, groups)
    norms = lax.all_to_all(norms, ("utt", "tm"), 0, 0, tiled=True)
    shares = shares[:1] + [
        lax.ppermute(shares[k], "utt", [(g, g ^ k) for g in range(groups)]) for k in range(1, groups)
    ]
    mean_grad = finish(scalars, band_coef, shares, norms, noise_draws, 300.0 * math.sqrt(width))
    return (block_out, mean_grad)


def solution(mesh):
    return jax.shard_map(
        per_device,
        mesh=mesh,
        in_specs=(
            P(("utt", "tm"), None),
            P(("utt", "tm"), None),
            P(),
            P(),
            P("tm", None),
            P("utt", None),
            P("utt", None),
            P(None, "utt", "tm"),
            P(),
        ),
        out_specs=(P(("utt", "tm"), None), P("utt", "tm")),
        check_vma=False,
    )
```
